32 devices in a mesh: seq: 16 (over z, y, x), tp: 2 (over core).
Axes of the slice: x: 2, y: 2, z: 4, core: 2. Of those that a mesh axis runs over, the one named last changes fastest.
Arguments:
- query_proj: bfloat16 [2048, 4096], P('seq', 'tp'), may hold values from -500 to 500
- key_proj: bfloat16 [2048, 4096], P('seq', 'tp'), may hold values from -500 to 500
- value_proj: bfloat16 [2048, 4096], P('seq', 'tp'), may hold values from -6 to 6
- query_gain: float32 [4096], P('tp'), may hold values from 0.5 to 1.5
- key_gain: float32 [4096], P('tp'), may hold values from 0.5 to 1.5
- live_tiles: int32 [32, 16, 4], P('tp'), may hold values from 0 to 15, as said below
- live_count: int32 [32, 16], P('tp'), may hold values from 1 to 4, as said below
Outputs:
- attended: bfloat16 [2048, 4096], P('seq', 'tp')
The draws below stay inside these ranges and needn't reach their ends.
Inputs may be any that keep to these rules, and one draw needn't show every extreme that they name: `live_tiles`: the entries of a row are distinct tiles and the first is the row's own tile; only the first live_count of them are used. `live_count`: every head has a query tile with 4 live key tiles.
All inputs are finite; a program needn't handle non-finite values.
Results may differ from the reference program's by a relative error of at most 0.012.
The reference program's roundings to bfloat16 on the way count: a program that leaves them out, or rounds other values in their place, can miss the bound.
Values may be sent and summed in bfloat16 or wider, within the bound.
No kernel may reach another device: no remote copies, remote signals or barrier semaphores. Data moves between devices by JAX's collectives and lax.ppermute only.
A program may use at most 128 MiB of HBM per device.

```python
import math
import jax
import jax.numpy as jnp
from jax import lax

HEAD_DIM = 128
HEADS = 32
TOK_DEV = 128
TILE = 128
FT = 24
QB = 4
TOKENS = 2048
MAXK = 4
N_SEQ = 16


def pair_fields(base_key):
    folded = jax.random.fold_in(base_key, 101)
    streams = jax.random.split(folded, 5)
    count = TOK_DEV * N_SEQ
    column_scale = 10.0 ** jax.random.uniform(streams[0], (HEADS, HEAD_DIM))
    query_rows = 10.0 ** jax.random.uniform(streams[1], (count,))
    key_rows = 10.0 ** jax.random.uniform(streams[2], (count,))
    full_shape = (count, HEADS, HEAD_DIM)
    query_noise = jnp.clip(jax.random.normal(streams[3], full_shape), -5.0, 5.0)
    key_noise = jnp.clip(jax.random.normal(streams[4], full_shape), -5.0, 5.0)
    query_field = query_noise * column_scale[None, :, :] * query_rows[:, None, None]
    key_field = key_noise * column_scale[None, :, :] * key_rows[:, None, None]
    query_field = query_field.reshape(count, HEADS * HEAD_DIM).astype(jnp.bfloat16)
    key_field = key_field.reshape(count, HEADS * HEAD_DIM).astype(jnp.bfloat16)
    return (query_field, key_field)


def tile_plan(base_key):
    folded = jax.random.fold_in(base_key, 202)
    streams = jax.random.split(folded, 5)
    tiles = TOK_DEV * N_SEQ // TILE
    index = jnp.arange(tiles, dtype=jnp.int32)
    spatial = jax.random.randint(streams[0], (HEADS,), 0, 2)
    same_frame = index[:, None] // FT == index[None, :] // FT
    offset = jnp.abs((index % FT)[:, None] - (index % FT)[None, :])
    same_place = offset <= 1
    wanted = jnp.where(spatial[:, None, None] == 1, same_frame[None], same_place[None]).astype(jnp.int32) * 2
    diagonal = (index[:, None] == index[None, :]).astype(jnp.int32) * 3
    wanted = jnp.maximum(wanted, diagonal[None])
    noise = jax.random.randint(streams[1], (HEADS, tiles, tiles), 0, tiles)
    score = wanted * tiles * tiles + noise * tiles + index[None, None, :]
    chosen = lax.top_k(score, MAXK)[1].astype(jnp.int32)
    region_size = max(1, min(FT, tiles // 4))
    regions = (tiles + region_size - 1) // region_size
    region_of = index // region_size
    hot = jax.random.randint(streams[2], (HEADS, regions), 0, 3) == 0
    forced = jax.random.randint(streams[3], (HEADS,), 0, regions)
    hot = hot | (jnp.arange(regions)[None, :] == forced[:, None])
    hot_tile = hot[:, region_of]
    baseline = jax.random.randint(streams[4], (HEADS, tiles), 1, MAXK // 2 + 1)
    counts = jnp.where(hot_tile, MAXK, baseline).astype(jnp.int32)
    return (chosen, counts)


def draw_query_proj(key, part):
    return pair_fields(key)[0]


def draw_key_proj(key, part):
    return pair_fields(key)[1]


def draw_live_tiles(key, part):
    return tile_plan(key)[0]


def draw_live_count(key, part):
    return tile_plan(key)[1]


def level_of(key, dims, pieces, least, high):
    def one(dim, blocks):
        draws = jax.random.uniform(jax.random.fold_in(jax.random.fold_in(key, 6), dim), (blocks,), jnp.float32, least / len(pieces), high / len(pieces))
        return jnp.repeat(jnp.exp(draws), dims[dim] // blocks).reshape((-1,) + (1,) * (len(dims) - dim - 1))

    level = one(*pieces[0])
    for cut in pieces[1:]:
        level = level * one(*cut)
    return level


def scatter_about(own_key, extent, spread, limit, shards=(), held_as=jnp.bfloat16):
    result = spread * jax.random.normal(own_key, extent, jnp.float32)
    if shards:
        result = result * level_of(own_key, extent, shards, -0.22, 0.18)
    return jnp.clip(result, -limit, limit).astype(held_as)


def setup_inputs(seed: int = 0) -> dict:
    seeds = jax.random.split(jax.random.key(seed), 8)
    return {
        "query_proj": draw_query_proj(jax.random.fold_in(seeds[7], 71), 0),
        "key_proj": draw_key_proj(jax.random.fold_in(seeds[7], 71), 0),
        "value_proj": scatter_about(seeds[2], (TOKENS, HEADS * HEAD_DIM), 1.0, 6.0, ((0, 16), (1, 2))),
        "query_gain": jnp.clip(1.0 + 0.1 * jax.random.normal(seeds[3], (HEADS * HEAD_DIM,), jnp.float32), 0.5, 1.5),
        "key_gain": jnp.clip(1.0 + 0.1 * jax.random.normal(seeds[4], (HEADS * HEAD_DIM,), jnp.float32), 0.5, 1.5),
        "live_tiles": draw_live_tiles(jax.random.fold_in(seeds[7], 71), 0),
        "live_count": draw_live_count(jax.random.fold_in(seeds[7], 71), 0),
    }


epsilon = 1e-06

def normalize(field, gain):
    values = field.astype(jnp.float32)
    squares = lax.optimization_barrier(jnp.sum(values * values, axis=1, keepdims=True))
    width = values.shape[1]
    return (values * lax.rsqrt(squares / width + epsilon) * gain[None, :]).astype(jnp.bfloat16)

def reference(query_proj, key_proj, value_proj, query_gain, key_gain, live_tiles, live_count):
    normed_query = normalize(query_proj, query_gain)
    normed_key = normalize(key_proj, key_gain)
    tile_count = query_proj.shape[0] // TILE
    score_scale = 1.0 / math.sqrt(HEAD_DIM)

    def split_heads(field):
        return field.reshape(tile_count, TILE, HEADS, HEAD_DIM).transpose(2, 0, 1, 3)
    query_tiles = split_heads(normed_query)
    key_tiles = split_heads(normed_key)
    value_tiles = split_heads(value_proj)

    def one_head(inputs):
        head_query, head_key, head_value, head_lists, head_counts = inputs

        def one_block(block):
            query_block_slice, block_lists, block_counts = block
            collected_key_rows = head_key[block_lists].reshape(QB, MAXK * TILE, HEAD_DIM)
            collected_value_rows = head_value[block_lists].reshape(QB, MAXK * TILE, HEAD_DIM)
            logit_scores = jnp.einsum('xzm,xym->xzy', query_block_slice.astype(jnp.float32), collected_key_rows.astype(jnp.float32)) * score_scale
            live_mask = jnp.arange(MAXK, dtype=jnp.int32)[None, :] < block_counts[:, None]
            live_mask = jnp.repeat(live_mask, TILE, axis=1)[:, None, :]
            largest = lax.optimization_barrier(jnp.max(jnp.where(live_mask, logit_scores, -jnp.inf), axis=-1, keepdims=True))
            weights = jnp.where(live_mask, jnp.exp(logit_scores - largest), 0.0)
            denominators = lax.optimization_barrier(jnp.sum(weights, axis=-1, keepdims=True))
            rounded_result = weights.astype(jnp.bfloat16)
            weighted_value_sum = jnp.einsum('ihp,ipe->ihe', rounded_result.astype(jnp.float32), collected_value_rows.astype(jnp.float32))
            return (weighted_value_sum / denominators).astype(jnp.bfloat16)
        return lax.map(one_block, (head_query.reshape(tile_count // QB, QB, TILE, HEAD_DIM), head_lists.reshape(tile_count // QB, QB, MAXK), head_counts.reshape(tile_count // QB, QB)))
    results = lax.map(one_head, (query_tiles, key_tiles, value_tiles, live_tiles, live_count))
    results = results.reshape(HEADS, tile_count, TILE, HEAD_DIM).transpose(1, 2, 0, 3)
    return results.reshape(tile_count * TILE, HEADS * HEAD_DIM)
```

```python
import functools
import math

import jax
import jax.numpy as jnp
from jax import lax
from jax.experimental import pallas as pl
from jax.experimental.pallas import tpu as pltpu
from jax.sharding import PartitionSpec as P

TILE = 128
LANES = 128
epsilon = 1e-06


def pack_kernel(query_ref, key_ref, value_ref, packed_ref, sems):
    heads, _, triple = packed_ref.shape
    width = triple // 3
    copies = []
    for place, source in enumerate((query_ref, key_ref, value_ref)):
        for head in range(heads):
            copies.append(
                pltpu.make_async_copy(
                    source.at[:, pl.ds(head * width, width)],
                    packed_ref.at[head, :, pl.ds(place * width, width)],
                    sems.at[place, head],
                )
            )
    for copy in copies:
        copy.start()
    for copy in copies:
        copy.wait()


def pack(query, key, value, heads):
    tokens, columns = query.shape
    return pl.pallas_call(
        pack_kernel,
        out_shape=jax.ShapeDtypeStruct((heads, tokens, 3 * columns // heads), query.dtype),
        in_specs=[pl.BlockSpec(memory_space=pl.ANY)] * 3,
        out_specs=pl.BlockSpec(memory_space=pl.ANY),
        scratch_shapes=[pltpu.SemaphoreType.DMA((3, heads))],
        name="pack_heads",
    )(query, key, value)


def unpack_kernel(heads_ref, out_ref, sems):
    heads, _, width = heads_ref.shape
    copies = [
        pltpu.make_async_copy(
            heads_ref.at[head], out_ref.at[:, pl.ds(head * width, width)], sems.at[head]
        )
        for head in range(heads)
    ]
    for copy in copies:
        copy.start()
    for copy in copies:
        copy.wait()


def unpack(by_head):
    heads, tokens, width = by_head.shape
    return pl.pallas_call(
        unpack_kernel,
        out_shape=jax.ShapeDtypeStruct((tokens, heads * width), by_head.dtype),
        in_specs=[pl.BlockSpec(memory_space=pl.ANY)],
        out_specs=pl.BlockSpec(memory_space=pl.ANY),
        scratch_shapes=[pltpu.SemaphoreType.DMA((heads,))],
        name="unpack_heads",
    )(by_head)


def attend_kernel(
    most_live, lists, counts, base, factors_ref, gains_ref, gathered_ref, out_ref, columns, normed_key
):
    head_width = out_ref.shape[2]
    tile_count = gathered_ref.shape[0] // TILE
    scale = math.log2(math.e) / math.sqrt(head_width)
    for block in range(columns.shape[0]):
        columns[block] = factors_ref[block * LANES : (block + 1) * LANES, :].T

    def column(which):
        lane = lax.broadcasted_iota(jnp.int32, (TILE, LANES), 1)
        block = columns[which // LANES]
        return jnp.sum(jnp.where(lane == which % LANES, block, 0.0), axis=1, keepdims=True)

    def normalize(rows, place, which):
        values = gathered_ref[rows, place * head_width : (place + 1) * head_width]
        values = values.astype(jnp.float32) * column(which) * gains_ref[place : place + 1, :]
        return values.astype(jnp.bfloat16)

    def rows_of(tile):
        return pl.ds(pl.multiple_of(tile * TILE, TILE), TILE)

    def key_step(tile, carry):
        normed_key[rows_of(tile), :] = normalize(rows_of(tile), 1, tile_count + tile)
        return carry

    lax.fori_loop(0, tile_count, key_step, 0, unroll=4)

    def query_step(step, carry):
        tile = base[0] + step
        query = normalize(rows_of(tile), 0, tile)
        live = [lists[step * most_live + slot] for slot in range(most_live)]
        count = counts[step]
        scores = []
        for slot in range(most_live):
            score = lax.dot_general(
                query,
                normed_key[rows_of(live[slot]), :],
                (((1,), (1,)), ((), ())),
                preferred_element_type=jnp.float32,
            )
            scores.append(score if slot == 0 else jnp.where(slot < count, score, -jnp.inf))
        largest = functools.reduce(jnp.maximum, scores)
        largest = jnp.max(largest, axis=1, keepdims=True)
        weights = [jnp.exp2((score - largest) * scale) for score in scores]
        denominators = jnp.sum(functools.reduce(jnp.add, weights), axis=1, keepdims=True)
        total = jnp.zeros((TILE, head_width), jnp.float32)
        for slot in range(most_live):
            total = total + jnp.dot(
                weights[slot].astype(jnp.bfloat16),
                gathered_ref[rows_of(live[slot]), 2 * head_width :],
                preferred_element_type=jnp.float32,
            )
        out_ref[step] = (total / denominators).astype(out_ref.dtype)
        return carry

    lax.fori_loop(0, out_ref.shape[0], query_step, 0, unroll=max(1, 8 // most_live))


def attend(gathered, factors, gains, lists, counts, base, tiles):
    head_width = gathered.shape[1] // 3
    most_live = lists.shape[1]
    tile_count = gathered.shape[0] // TILE
    blocks = -(-factors.shape[0] // LANES)
    factors = jnp.pad(factors, ((0, blocks * LANES - factors.shape[0]), (0, 0)))
    smem = pl.BlockSpec(memory_space=pltpu.SMEM)
    vmem = pl.BlockSpec(memory_space=pltpu.VMEM)
    return pl.pallas_call(
        functools.partial(attend_kernel, most_live),
        out_shape=jax.ShapeDtypeStruct((tiles, TILE, head_width), jnp.bfloat16),
        in_specs=[smem] * 3 + [vmem] * 3,
        out_specs=vmem,
        scratch_shapes=[
            pltpu.VMEM((blocks, LANES, LANES), jnp.float32),
            pltpu.VMEM((tile_count * TILE, head_width), jnp.bfloat16),
        ],
        compiler_params=pltpu.CompilerParams(vmem_limit_bytes=48 * 1024 * 1024),
        name="attend",
    )(lists.reshape(-1), counts, base, factors, gains, gathered)


def gather_over(values, axis):
    count = lax.axis_size(axis)
    if count & (count - 1):
        return lax.all_gather(values, axis)
    me = lax.axis_index(axis)
    held = values[None]
    reach = 1
    while reach < count:
        other = lax.ppermute(held, axis, [(i, i ^ reach) for i in range(count)])
        upper = (me & reach) != 0
        held = jnp.where(
            upper, jnp.concatenate([other, held], 0), jnp.concatenate([held, other], 0)
        )
        reach *= 2
    return held


def local(query_proj, key_proj, value_proj, query_gain, key_gain, live_tiles, live_count):
    tokens_here = query_proj.shape[0]
    heads_here = live_tiles.shape[0]
    head_width = query_proj.shape[1] // heads_here
    full_width = query_proj.shape[1] * lax.axis_size("tp")
    device_count = lax.axis_size("seq")
    group_size = device_count // heads_here
    my_index = lax.axis_index("seq")
    my_head = my_index // group_size
    my_member = my_index % group_size

    outgoing = pack(query_proj, key_proj, value_proj, heads_here)
    if group_size > 1:
        outgoing = jnp.repeat(outgoing, group_size, axis=0)
    incoming = lax.all_to_all(outgoing, "seq", split_axis=0, concat_axis=0, tiled=True)
    gathered = incoming.reshape(device_count * tokens_here, 3 * head_width)

    query_values = query_proj.astype(jnp.float32)
    key_values = key_proj.astype(jnp.float32)
    squares = jnp.stack(
        [jnp.sum(query_values * query_values, axis=1), jnp.sum(key_values * key_values, axis=1)]
    )
    squares = lax.psum(squares, "tp")
    factors = gather_over(lax.rsqrt(squares / full_width + epsilon), "seq")
    tile_count = device_count * tokens_here // TILE
    factors = factors.transpose(1, 0, 2).reshape(2 * tile_count, TILE)
    gains = jnp.stack([query_gain, key_gain]).reshape(2, heads_here, head_width)
    gains = lax.dynamic_index_in_dim(gains, my_head, 1, keepdims=False)

    per_member = tile_count // group_size
    base = my_member * per_member
    lists = lax.dynamic_index_in_dim(live_tiles, my_head, 0, keepdims=False)
    counts = lax.dynamic_index_in_dim(live_count, my_head, 0, keepdims=False)
    lists = lax.dynamic_slice_in_dim(lists, base, per_member, 0)
    counts = lax.dynamic_slice_in_dim(counts, base, per_member, 0)
    results = attend(
        gathered, factors, gains, lists, counts, base.astype(jnp.int32).reshape(1), per_member
    )
    if group_size > 1:
        placed = jnp.zeros((tile_count, TILE, head_width), jnp.bfloat16)
        results = lax.dynamic_update_slice_in_dim(placed, results, base, 0)
    results = results.reshape(device_count, tokens_here, head_width)
    returned = lax.all_to_all(results, "seq", split_axis=0, concat_axis=0, tiled=True)
    if group_size > 1:
        returned = returned.reshape(heads_here, group_size, tokens_here, head_width)
        returned = returned.astype(jnp.float32).sum(axis=1).astype(jnp.bfloat16)
    return unpack(returned)


def solution(mesh):
    placed = (
        P("seq", "tp"),
        P("seq", "tp"),
        P("seq", "tp"),
        P("tp"),
        P("tp"),
        P("tp", None, None),
        P("tp", None),
    )
    return jax.shard_map(
        local, mesh=mesh, in_specs=placed, out_specs=P("seq", "tp"), check_vma=False
    )
```

```python
import functools
import math

import jax
import jax.numpy as jnp
from jax import lax
from jax.experimental import pallas as pl
from jax.experimental.pallas import tpu as pltpu
from jax.sharding import PartitionSpec as P

TILE = 128
LANES = 128
UNROLL = 16
epsilon = 1e-06


def attend_kernel(
    most_live,
    lists_hbm,
    counts_hbm,
    factors_ref,
    gains_ref,
    gathered_ref,
    out_ref,
    lists,
    counts,
    columns,
    normed_query,
    normed_key,
    scores,
    weights,
    rows_kept,
    sems,
):
    head_width = out_ref.shape[2]
    tiles = out_ref.shape[0]
    tile_count = gathered_ref.shape[0] // TILE
    together = scores.shape[0]
    scale = math.log2(math.e) / math.sqrt(head_width)
    to_smem = [
        pltpu.make_async_copy(lists_hbm, lists, sems.at[0]),
        pltpu.make_async_copy(counts_hbm, counts, sems.at[1]),
    ]
    for copy in to_smem:
        copy.start()
    for block in range(columns.shape[0]):
        columns[block] = factors_ref[block * LANES : (block + 1) * LANES, :].T

    def rows_of(tile):
        return pl.ds(pl.multiple_of(tile * TILE, TILE), TILE)

    def each(count, step):
        if count <= UNROLL:
            for index in range(count):
                step(index)
        else:

            def body(index, carry):
                step(index)
                return carry

            lax.fori_loop(0, count, body, 0)

    def normalize(tile, place, which):
        lane = lax.broadcasted_iota(jnp.int32, (TILE, LANES), 1)
        column = jnp.sum(
            jnp.where(lane == which % LANES, columns[which // LANES], 0.0), axis=1, keepdims=True
        )
        values = gathered_ref[rows_of(tile), place * head_width : (place + 1) * head_width]
        values = values.astype(jnp.float32) * column * gains_ref[place : place + 1, :]
        return values.astype(jnp.bfloat16)

    def normalize_step(tile):
        normed_query[rows_of(tile), :] = normalize(tile, 0, tile)
        normed_key[rows_of(tile), :] = normalize(tile, 1, tile_count + tile)

    each(tile_count, normalize_step)
    for copy in to_smem:
        copy.wait()
    base = counts[tiles]

    def live_of(step):
        return [lists[step * most_live + slot] for slot in range(most_live)]

    def some_tiles(first):
        for place in range(together):
            step = first + place
            keys = [normed_key[rows_of(live), :] for live in live_of(step)]
            score = lax.dot_general(
                normed_query[rows_of(base + step), :],
                jnp.concatenate(keys, axis=0),
                (((1,), (1,)), ((), ())),
                preferred_element_type=jnp.float32,
            )
            slot = lax.broadcasted_iota(jnp.int32, (1, most_live * TILE), 1) // TILE
            score = jnp.where(slot < counts[step], score, -jnp.inf)
            scores[place] = score
            largest = jnp.max(score, axis=1, keepdims=True)
            rows_kept[place] = jnp.broadcast_to(largest, (TILE, LANES))
        for place in range(together):
            largest = jnp.concatenate([rows_kept[place]] * most_live, axis=1)
            weight = jnp.exp2((scores[place] - largest) * scale)
            weights[place] = weight.astype(jnp.bfloat16)
            denominators = jnp.sum(weight, axis=1, keepdims=True)
            rows_kept[place] = jnp.broadcast_to(denominators, (TILE, LANES))
        for place in range(together):
            step = first + place
            values = [gathered_ref[rows_of(live), 2 * head_width :] for live in live_of(step)]
            total = jnp.dot(
                weights[place],
                jnp.concatenate(values, axis=0),
                preferred_element_type=jnp.float32,
            )
            out_ref[step] = (total / rows_kept[place]).astype(out_ref.dtype)

    if tiles == together:
        some_tiles(0)
    else:

        def several(index, carry):
            some_tiles(index * together)
            return carry

        lax.fori_loop(0, tiles // together, several, 0)


def attend(gathered, factors, gains, lists, counts, base, tiles):
    head_width = gathered.shape[1] // 3
    most_live = lists.shape[1]
    tile_count = gathered.shape[0] // TILE
    blocks = -(-factors.shape[0] // LANES)
    factors = jnp.pad(factors, ((0, blocks * LANES - factors.shape[0]), (0, 0)))
    lists = lists.reshape(-1)
    counts = jnp.concatenate([counts, base.reshape(1)])
    together = max(size for size in range(1, max(1, 64 // most_live) + 1) if tiles % size == 0)
    anywhere = pl.BlockSpec(memory_space=pl.ANY)
    vmem = pl.BlockSpec(memory_space=pltpu.VMEM)
    return pl.pallas_call(
        functools.partial(attend_kernel, most_live),
        out_shape=jax.ShapeDtypeStruct((tiles, TILE, head_width), jnp.bfloat16),
        in_specs=[anywhere] * 2 + [vmem] * 3,
        out_specs=vmem,
        scratch_shapes=[
            pltpu.SMEM(lists.shape, jnp.int32),
            pltpu.SMEM(counts.shape, jnp.int32),
            pltpu.VMEM((blocks, LANES, LANES), jnp.float32),
            pltpu.VMEM((tile_count * TILE, head_width), jnp.bfloat16),
            pltpu.VMEM((tile_count * TILE, head_width), jnp.bfloat16),
            pltpu.VMEM((together, TILE, most_live * TILE), jnp.float32),
            pltpu.VMEM((together, TILE, most_live * TILE), jnp.bfloat16),
            pltpu.VMEM((together, TILE, LANES), jnp.float32),
            pltpu.SemaphoreType.DMA((2,)),
        ],
        compiler_params=pltpu.CompilerParams(vmem_limit_bytes=48 * 1024 * 1024),
        name="attend",
    )(lists, counts, factors, gains, gathered)


def gather_over(values, axis):
    count = lax.axis_size(axis)
    if count & (count - 1):
        return lax.all_gather(values, axis)
    me = lax.axis_index(axis)
    held = values[None]
    block = count
    while block > 1:
        radix = 4 if block % 4 == 0 else 2
        block //= radix
        others = [
            lax.ppermute(held, axis, [(i, i ^ (turn * block)) for i in range(count)])
            for turn in range(1, radix)
        ]
        parts = [held] + others
        mine = (me // block) % radix
        ordered = []
        for place in range(radix):
            part = parts[0]
            for turn in range(1, radix):
                part = jnp.where((mine ^ place) == turn, parts[turn], part)
            ordered.append(part)
        held = jnp.stack(ordered, axis=-1 - values.ndim)
        held = held.reshape((-1,) + values.shape)
    return held


def local(query_proj, key_proj, value_proj, query_gain, key_gain, live_tiles, live_count):
    tokens_here = query_proj.shape[0]
    heads_here = live_tiles.shape[0]
    head_width = query_proj.shape[1] // heads_here
    full_width = query_proj.shape[1] * lax.axis_size("tp")
    device_count = lax.axis_size("seq")
    group_size = device_count // heads_here
    my_index = lax.axis_index("seq")
    my_head = my_index // group_size
    my_member = my_index % group_size

    outgoing = jnp.concatenate(
        [
            field.reshape(tokens_here, heads_here, head_width)
            for field in (query_proj, key_proj, value_proj)
        ],
        axis=2,
    ).transpose(1, 0, 2)
    if group_size > 1:
        outgoing = jnp.repeat(outgoing, group_size, axis=0)
    incoming = lax.all_to_all(outgoing, "seq", split_axis=0, concat_axis=0, tiled=True)
    gathered = incoming.reshape(device_count * tokens_here, 3 * head_width)

    query_values = query_proj.astype(jnp.float32)
    key_values = key_proj.astype(jnp.float32)
    squares = jnp.stack(
        [jnp.sum(query_values * query_values, axis=1), jnp.sum(key_values * key_values, axis=1)]
    )
    squares = lax.psum(squares, "tp")
    factors = gather_over(lax.rsqrt(squares / full_width + epsilon), "seq")
    tile_count = device_count * tokens_here // TILE
    factors = factors.transpose(1, 0, 2).reshape(2 * tile_count, TILE)
    gains = jnp.stack([query_gain, key_gain]).reshape(2, heads_here, head_width)
    gains = lax.dynamic_index_in_dim(gains, my_head, 1, keepdims=False)

    per_member = tile_count // group_size
    base = my_member * per_member
    lists = lax.dynamic_index_in_dim(live_tiles, my_head, 0, keepdims=False)
    counts = lax.dynamic_index_in_dim(live_count, my_head, 0, keepdims=False)
    lists = lax.dynamic_slice_in_dim(lists, base, per_member, 0)
    counts = lax.dynamic_slice_in_dim(counts, base, per_member, 0)
    results = attend(
        gathered, factors, gains, lists, counts, base.astype(jnp.int32), per_member
    )
    if group_size > 1:
        placed = jnp.zeros((tile_count, TILE, head_width), jnp.bfloat16)
        results = lax.dynamic_update_slice_in_dim(placed, results, base, 0)
    results = results.reshape(device_count, tokens_here, head_width)
    returned = lax.all_to_all(results, "seq", split_axis=0, concat_axis=0, tiled=True)
    if group_size > 1:
        returned = returned.reshape(heads_here, group_size, tokens_here, head_width)
        returned = returned.astype(jnp.float32).sum(axis=1).astype(jnp.bfloat16)
    return returned.transpose(1, 0, 2).reshape(tokens_here, heads_here * head_width)


def solution(mesh):
    placed = (
        P("seq", "tp"),
        P("seq", "tp"),
        P("seq", "tp"),
        P("tp"),
        P("tp"),
        P("tp", None, None),
        P("tp", None),
    )
    return jax.shard_map(
        local, mesh=mesh, in_specs=placed, out_specs=P("seq", "tp"), check_vma=False
    )
```

```python
import functools
import math

import jax
import jax.numpy as jnp
from jax import lax
from jax.experimental import pallas as pl
from jax.experimental.pallas import tpu as pltpu
from jax.sharding import PartitionSpec as P

TILE = 128
LANES = 128
epsilon = 1e-06


def pack_kernel(query_ref, key_ref, value_ref, factors_ref, gains_ref, packed_ref):
    heads, tokens, triple = packed_ref.shape
    width = triple // 3
    for first in range(0, tokens, LANES):
        rows = slice(first, first + LANES)
        for place, field_ref in enumerate((query_ref, key_ref)):
            factor = jnp.broadcast_to(factors_ref[place : place + 1, rows], (width, LANES)).T
            for head in range(heads):
                columns = slice(head * width, (head + 1) * width)
                values = field_ref[rows, columns].astype(jnp.float32) * factor
                values = values * gains_ref[place : place + 1, columns]
                packed_ref[head, rows, place * width : (place + 1) * width] = values.astype(
                    packed_ref.dtype
                )
    for head in range(heads):
        packed_ref[head, :, 2 * width :] = value_ref[:, head * width : (head + 1) * width]


def pack(query, key, value, factors, gains, heads):
    tokens, columns = query.shape
    vmem = pl.BlockSpec(memory_space=pltpu.VMEM)
    return pl.pallas_call(
        pack_kernel,
        out_shape=jax.ShapeDtypeStruct((heads, tokens, 3 * columns // heads), query.dtype),
        in_specs=[vmem] * 5,
        out_specs=vmem,
        compiler_params=pltpu.CompilerParams(vmem_limit_bytes=16 * 1024 * 1024),
        name="normalize_and_pack",
    )(query, key, value, factors, gains)


def attend_kernel(
    most_live,
    lists_hbm,
    counts_hbm,
    gathered_ref,
    out_ref,
    lists,
    counts,
    scores,
    weights,
    rows_kept,
    sems,
):
    head_width = out_ref.shape[2]
    tiles = out_ref.shape[0]
    together = scores.shape[0]
    scale = math.log2(math.e) / math.sqrt(head_width)
    to_smem = [
        pltpu.make_async_copy(lists_hbm, lists, sems.at[0]),
        pltpu.make_async_copy(counts_hbm, counts, sems.at[1]),
    ]
    for copy in to_smem:
        copy.start()
    for copy in to_smem:
        copy.wait()
    base = counts[tiles]

    def part(tile, place):
        rows = pl.ds(pl.multiple_of(tile * TILE, TILE), TILE)
        return gathered_ref[rows, place * head_width : (place + 1) * head_width]

    def live_parts(step, place):
        live = [lists[step * most_live + slot] for slot in range(most_live)]
        return jnp.concatenate([part(tile, place) for tile in live], axis=0)

    def some_tiles(first):
        for place in range(together):
            step = first + place
            score = lax.dot_general(
                part(base + step, 0),
                live_parts(step, 1),
                (((1,), (1,)), ((), ())),
                preferred_element_type=jnp.float32,
            )
            slot = lax.broadcasted_iota(jnp.int32, (1, most_live * TILE), 1) // TILE
            score = jnp.where(slot < counts[step], score, -jnp.inf)
            scores[place] = score
            largest = jnp.max(score, axis=1, keepdims=True)
            rows_kept[place] = jnp.broadcast_to(largest, (TILE, LANES))
        for place in range(together):
            largest = jnp.concatenate([rows_kept[place]] * most_live, axis=1)
            weight = jnp.exp2((scores[place] - largest) * scale)
            weights[place] = weight.astype(jnp.bfloat16)
            denominators = jnp.sum(weight, axis=1, keepdims=True)
            rows_kept[place] = jnp.broadcast_to(denominators, (TILE, LANES))
        for place in range(together):
            step = first + place
            total = jnp.dot(
                weights[place], live_parts(step, 2), preferred_element_type=jnp.float32
            )
            out_ref[step] = (total / rows_kept[place]).astype(out_ref.dtype)

    if tiles == together:
        some_tiles(0)
    else:

        def several(index, carry):
            some_tiles(index * together)
            return carry

        lax.fori_loop(0, tiles // together, several, 0)


def attend(gathered, lists, counts, base, tiles):
    head_width = gathered.shape[1] // 3
    most_live = lists.shape[1]
    lists = lists.reshape(-1)
    counts = jnp.concatenate([counts, base.reshape(1)])
    together = max(size for size in range(1, max(1, 64 // most_live) + 1) if tiles % size == 0)
    anywhere = pl.BlockSpec(memory_space=pl.ANY)
    vmem = pl.BlockSpec(memory_space=pltpu.VMEM)
    return pl.pallas_call(
        functools.partial(attend_kernel, most_live),
        out_shape=jax.ShapeDtypeStruct((tiles, TILE, head_width), jnp.bfloat16),
        in_specs=[anywhere] * 2 + [vmem],
        out_specs=vmem,
        scratch_shapes=[
            pltpu.SMEM(lists.shape, jnp.int32),
            pltpu.SMEM(counts.shape, jnp.int32),
            pltpu.VMEM((together, TILE, most_live * TILE), jnp.float32),
            pltpu.VMEM((together, TILE, most_live * TILE), jnp.bfloat16),
            pltpu.VMEM((together, TILE, LANES), jnp.float32),
            pltpu.SemaphoreType.DMA((2,)),
        ],
        compiler_params=pltpu.CompilerParams(vmem_limit_bytes=40 * 1024 * 1024),
        name="attend",
    )(lists, counts, gathered)


def local(query_proj, key_proj, value_proj, query_gain, key_gain, live_tiles, live_count):
    tokens_here = query_proj.shape[0]
    heads_here = live_tiles.shape[0]
    head_width = query_proj.shape[1] // heads_here
    full_width = query_proj.shape[1] * lax.axis_size("tp")
    device_count = lax.axis_size("seq")
    group_size = device_count // heads_here
    my_index = lax.axis_index("seq")
    my_head = my_index // group_size
    my_member = my_index % group_size

    query_values = query_proj.astype(jnp.float32)
    key_values = key_proj.astype(jnp.float32)
    squares = jnp.stack(
        [jnp.sum(query_values * query_values, axis=1), jnp.sum(key_values * key_values, axis=1)]
    )
    squares = lax.psum(squares, "tp")
    factors = lax.rsqrt(squares / full_width + epsilon)
    gains = jnp.stack([query_gain, key_gain])
    outgoing = pack(query_proj, key_proj, value_proj, factors, gains, heads_here)
    if group_size > 1:
        outgoing = jnp.repeat(outgoing, group_size, axis=0)
    incoming = lax.all_to_all(outgoing, "seq", split_axis=0, concat_axis=0, tiled=True)
    gathered = incoming.reshape(device_count * tokens_here, 3 * head_width)

    tile_count = device_count * tokens_here // TILE
    per_member = tile_count // group_size
    base = my_member * per_member
    lists = lax.dynamic_index_in_dim(live_tiles, my_head, 0, keepdims=False)
    counts = lax.dynamic_index_in_dim(live_count, my_head, 0, keepdims=False)
    lists = lax.dynamic_slice_in_dim(lists, base, per_member, 0)
    counts = lax.dynamic_slice_in_dim(counts, base, per_member, 0)
    results = attend(gathered, lists, counts, base.astype(jnp.int32), per_member)
    if group_size > 1:
        placed = jnp.zeros((tile_count, TILE, head_width), jnp.bfloat16)
        results = lax.dynamic_update_slice_in_dim(placed, results, base, 0)
    results = results.reshape(device_count, tokens_here, head_width)
    returned = lax.all_to_all(results, "seq", split_axis=0, concat_axis=0, tiled=True)
    if group_size > 1:
        returned = returned.reshape(heads_here, group_size, tokens_here, head_width)
        returned = returned.astype(jnp.float32).sum(axis=1).astype(jnp.bfloat16)
    return returned.transpose(1, 0, 2).reshape(tokens_here, heads_here * head_width)


def solution(mesh):
    placed = (
        P("seq", "tp"),
        P("seq", "tp"),
        P("seq", "tp"),
        P("tp"),
        P("tp"),
        P("tp", None, None),
        P("tp", None),
    )
    return jax.shard_map(
        local, mesh=mesh, in_specs=placed, out_specs=P("seq", "tp"), check_vma=False
    )
```

```python
import functools
import math

import jax
import jax.numpy as jnp
from jax import lax
from jax.experimental import pallas as pl
from jax.experimental.pallas import tpu as pltpu
from jax.sharding import PartitionSpec as P

TILE = 128
LANES = 128
UNROLL = 16
epsilon = 1e-06


def pack_kernel(query_hbm, key_hbm, value_hbm, packed_ref, query, key, value, sems):
    heads, _, triple = packed_ref.shape
    width = triple // 3
    held = (query, key, value)
    copies = [
        pltpu.make_async_copy(source, target, sems.at[place])
        for place, (source, target) in enumerate(zip((query_hbm, key_hbm, value_hbm), held))
    ]
    for copy in copies:
        copy.start()
    for place, field in enumerate(held):
        copies[place].wait()
        for head in range(heads):
            packed_ref[head, :, place * width : (place + 1) * width] = field[
                :, head * width : (head + 1) * width
            ]


def pack(query, key, value, heads):
    tokens, columns = query.shape
    return pl.pallas_call(
        pack_kernel,
        out_shape=jax.ShapeDtypeStruct((heads, tokens, 3 * columns // heads), query.dtype),
        in_specs=[pl.BlockSpec(memory_space=pl.ANY)] * 3,
        out_specs=pl.BlockSpec(memory_space=pltpu.VMEM),
        scratch_shapes=[pltpu.VMEM((tokens, columns), query.dtype)] * 3
        + [pltpu.SemaphoreType.DMA((3,))],
        compiler_params=pltpu.CompilerParams(vmem_limit_bytes=56 * 1024 * 1024),
        name="pack_heads",
    )(query, key, value)


def attend_kernel(
    most_live,
    lists_hbm,
    counts_hbm,
    factors_ref,
    gains_ref,
    gathered_ref,
    out_ref,
    lists,
    counts,
    columns,
    normed_query,
    normed_key,
    scores,
    weights,
    rows_kept,
    sems,
):
    head_width = out_ref.shape[2]
    tiles = out_ref.shape[0]
    tile_count = gathered_ref.shape[0] // TILE
    together = scores.shape[0]
    scale = math.log2(math.e) / math.sqrt(head_width)
    to_smem = [
        pltpu.make_async_copy(lists_hbm, lists, sems.at[0]),
        pltpu.make_async_copy(counts_hbm, counts, sems.at[1]),
    ]
    for copy in to_smem:
        copy.start()
    for block in range(columns.shape[0]):
        columns[block] = factors_ref[block * LANES : (block + 1) * LANES, :].T

    def rows_of(tile):
        return pl.ds(pl.multiple_of(tile * TILE, TILE), TILE)

    def each(count, step):
        if count <= UNROLL:
            for index in range(count):
                step(index)
        else:

            def body(index, carry):
                step(index)
                return carry

            lax.fori_loop(0, count, body, 0)

    def normalize(tile, place, which):
        lane = lax.broadcasted_iota(jnp.int32, (TILE, LANES), 1)
        column = jnp.sum(
            jnp.where(lane == which % LANES, columns[which // LANES], 0.0), axis=1, keepdims=True
        )
        values = gathered_ref[rows_of(tile), place * head_width : (place + 1) * head_width]
        values = values.astype(jnp.float32) * column * gains_ref[place : place + 1, :]
        return values.astype(jnp.bfloat16)

    def normalize_step(tile):
        normed_query[rows_of(tile), :] = normalize(tile, 0, tile)
        normed_key[rows_of(tile), :] = normalize(tile, 1, tile_count + tile)

    each(tile_count, normalize_step)
    for copy in to_smem:
        copy.wait()
    base = counts[tiles]

    def live_of(step):
        return [lists[step * most_live + slot] for slot in range(most_live)]

    def some_tiles(first):
        for place in range(together):
            step = first + place
            keys = [normed_key[rows_of(live), :] for live in live_of(step)]
            score = lax.dot_general(
                normed_query[rows_of(base + step), :],
                jnp.concatenate(keys, axis=0),
                (((1,), (1,)), ((), ())),
                preferred_element_type=jnp.float32,
            )
            slot = lax.broadcasted_iota(jnp.int32, (1, most_live * TILE), 1) // TILE
            score = jnp.where(slot < counts[step], score, -jnp.inf)
            scores[place] = score
            largest = jnp.max(score, axis=1, keepdims=True)
            rows_kept[place] = jnp.broadcast_to(largest, (TILE, LANES))
        for place in range(together):
            largest = jnp.concatenate([rows_kept[place]] * most_live, axis=1)
            weight = jnp.exp2((scores[place] - largest) * scale)
            weights[place] = weight.astype(jnp.bfloat16)
            denominators = jnp.sum(weight, axis=1, keepdims=True)
            rows_kept[place] = jnp.broadcast_to(denominators, (TILE, LANES))
        for place in range(together):
            step = first + place
            values = [gathered_ref[rows_of(live), 2 * head_width :] for live in live_of(step)]
            total = jnp.dot(
                weights[place],
                jnp.concatenate(values, axis=0),
                preferred_element_type=jnp.float32,
            )
            out_ref[step] = (total / rows_kept[place]).astype(out_ref.dtype)

    if tiles == together:
        some_tiles(0)
    else:

        def several(index, carry):
            some_tiles(index * together)
            return carry

        lax.fori_loop(0, tiles // together, several, 0)


def attend(gathered, factors, gains, lists, counts, base, tiles):
    head_width = gathered.shape[1] // 3
    most_live = lists.shape[1]
    tile_count = gathered.shape[0] // TILE
    blocks = -(-factors.shape[0] // LANES)
    factors = jnp.pad(factors, ((0, blocks * LANES - factors.shape[0]), (0, 0)))
    lists = lists.reshape(-1)
    counts = jnp.concatenate([counts, base.reshape(1)])
    together = max(size for size in range(1, max(1, 64 // most_live) + 1) if tiles % size == 0)
    anywhere = pl.BlockSpec(memory_space=pl.ANY)
    vmem = pl.BlockSpec(memory_space=pltpu.VMEM)
    return pl.pallas_call(
        functools.partial(attend_kernel, most_live),
        out_shape=jax.ShapeDtypeStruct((tiles, TILE, head_width), jnp.bfloat16),
        in_specs=[anywhere] * 2 + [vmem] * 3,
        out_specs=vmem,
        scratch_shapes=[
            pltpu.SMEM(lists.shape, jnp.int32),
            pltpu.SMEM(counts.shape, jnp.int32),
            pltpu.VMEM((blocks, LANES, LANES), jnp.float32),
            pltpu.VMEM((tile_count * TILE, head_width), jnp.bfloat16),
            pltpu.VMEM((tile_count * TILE, head_width), jnp.bfloat16),
            pltpu.VMEM((together, TILE, most_live * TILE), jnp.float32),
            pltpu.VMEM((together, TILE, most_live * TILE), jnp.bfloat16),
            pltpu.VMEM((together, TILE, LANES), jnp.float32),
            pltpu.SemaphoreType.DMA((2,)),
        ],
        compiler_params=pltpu.CompilerParams(vmem_limit_bytes=48 * 1024 * 1024),
        name="attend",
    )(lists, counts, factors, gains, gathered)


def gather_over(values, axis):
    count = lax.axis_size(axis)
    if count & (count - 1):
        return lax.all_gather(values, axis)
    me = lax.axis_index(axis)
    held = values[None]
    reach = 1
    while reach < count:
        other = lax.ppermute(held, axis, [(i, i ^ reach) for i in range(count)])
        upper = (me & reach) != 0
        held = jnp.where(
            upper, jnp.concatenate([other, held], 0), jnp.concatenate([held, other], 0)
        )
        reach *= 2
    return held


def local(query_proj, key_proj, value_proj, query_gain, key_gain, live_tiles, live_count):
    tokens_here = query_proj.shape[0]
    heads_here = live_tiles.shape[0]
    head_width = query_proj.shape[1] // heads_here
    full_width = query_proj.shape[1] * lax.axis_size("tp")
    device_count = lax.axis_size("seq")
    group_size = device_count // heads_here
    my_index = lax.axis_index("seq")
    my_head = my_index // group_size
    my_member = my_index % group_size

    outgoing = pack(query_proj, key_proj, value_proj, heads_here)
    if group_size > 1:
        outgoing = jnp.repeat(outgoing, group_size, axis=0)
    incoming = lax.all_to_all(outgoing, "seq", split_axis=0, concat_axis=0, tiled=True)
    gathered = incoming.reshape(device_count * tokens_here, 3 * head_width)

    query_values = query_proj.astype(jnp.float32)
    key_values = key_proj.astype(jnp.float32)
    squares = jnp.stack(
        [jnp.sum(query_values * query_values, axis=1), jnp.sum(key_values * key_values, axis=1)]
    )
    squares = lax.psum(squares, "tp")
    factors = gather_over(lax.rsqrt(squares / full_width + epsilon), "seq")
    tile_count = device_count * tokens_here // TILE
    factors = factors.transpose(1, 0, 2).reshape(2 * tile_count, TILE)
    gains = jnp.stack([query_gain, key_gain]).reshape(2, heads_here, head_width)
    gains = lax.dynamic_index_in_dim(gains, my_head, 1, keepdims=False)

    per_member = tile_count // group_size
    base = my_member * per_member
    lists = lax.dynamic_index_in_dim(live_tiles, my_head, 0, keepdims=False)
    counts = lax.dynamic_index_in_dim(live_count, my_head, 0, keepdims=False)
    lists = lax.dynamic_slice_in_dim(lists, base, per_member, 0)
    counts = lax.dynamic_slice_in_dim(counts, base, per_member, 0)
    results = attend(
        gathered, factors, gains, lists, counts, base.astype(jnp.int32), per_member
    )
    if group_size > 1:
        placed = jnp.zeros((tile_count, TILE, head_width), jnp.bfloat16)
        results = lax.dynamic_update_slice_in_dim(placed, results, base, 0)
    results = results.reshape(device_count, tokens_here, head_width)
    returned = lax.all_to_all(results, "seq", split_axis=0, concat_axis=0, tiled=True)
    if group_size > 1:
        returned = returned.reshape(heads_here, group_size, tokens_here, head_width)
        returned = returned.astype(jnp.float32).sum(axis=1).astype(jnp.bfloat16)
    return returned.transpose(1, 0, 2).reshape(tokens_here, heads_here * head_width)


def solution(mesh):
    placed = (
        P("seq", "tp"),
        P("seq", "tp"),
        P("seq", "tp"),
        P("tp"),
        P("tp"),
        P("tp", None, None),
        P("tp", None),
    )
    return jax.shard_map(
        local, mesh=mesh, in_specs=placed, out_specs=P("seq", "tp"), check_vma=False
    )
```

```python
import functools
import math

import jax
import jax.numpy as jnp
from jax import lax
from jax.experimental import pallas as pl
from jax.experimental.pallas import tpu as pltpu
from jax.sharding import PartitionSpec as P

TILE = 128
LANES = 128
UNROLL = 16
APART = 4
epsilon = 1e-06


def pack_kernel(
    query_hbm, key_hbm, value_hbm, packed_hbm, query, key, value, packed, fetched, written
):
    heads, _, _, width = packed.shape
    pieces = written.shape[1]
    fields = ((query_hbm, query), (key_hbm, key), (value_hbm, value))
    fetches = [
        pltpu.make_async_copy(source, target, fetched.at[place])
        for place, (source, target) in enumerate(fields)
    ]
    for fetch in fetches:
        fetch.start()
    writes = []
    for place, (_, field) in enumerate(fields):
        fetches[place].wait()
        for piece in range(pieces):
            some = range(piece * heads // pieces, (piece + 1) * heads // pieces)
            for head in some:
                packed[head, place] = field[:, head * width : (head + 1) * width]
            span = pl.ds(some[0], len(some))
            writes.append(
                pltpu.make_async_copy(
                    packed.at[span, place], packed_hbm.at[span, place], written.at[place, piece]
                )
            )
            writes[-1].start()
    for write in writes:
        write.wait()


def pack(query, key, value, heads):
    tokens, columns = query.shape
    shape = (heads, 3, tokens, columns // heads)
    anywhere = pl.BlockSpec(memory_space=pl.ANY)
    return pl.pallas_call(
        pack_kernel,
        out_shape=jax.ShapeDtypeStruct(shape, query.dtype),
        in_specs=[anywhere] * 3,
        out_specs=anywhere,
        scratch_shapes=[pltpu.VMEM((tokens, columns), query.dtype)] * 3
        + [
            pltpu.VMEM(shape, query.dtype),
            pltpu.SemaphoreType.DMA((3,)),
            pltpu.SemaphoreType.DMA((3, 2 if heads % 2 == 0 else 1)),
        ],
        compiler_params=pltpu.CompilerParams(vmem_limit_bytes=56 * 1024 * 1024),
        name="pack_heads",
    )(query, key, value)


def attend_kernel(
    most_live,
    lists_hbm,
    counts_hbm,
    factors_ref,
    gains_ref,
    gathered_ref,
    out_ref,
    lists,
    counts,
    columns,
    normed_query,
    normed_key,
    scores,
    weights,
    rows_kept,
    sems,
):
    head_width = out_ref.shape[2]
    tiles = out_ref.shape[0]
    here = gathered_ref.shape[2] // TILE
    tile_count = gathered_ref.shape[0] * here
    together = scores.shape[0]
    scale = math.log2(math.e) / math.sqrt(head_width)
    to_smem = [
        pltpu.make_async_copy(lists_hbm, lists, sems.at[0]),
        pltpu.make_async_copy(counts_hbm, counts, sems.at[1]),
    ]
    for copy in to_smem:
        copy.start()
    for block in range(columns.shape[0]):
        columns[block] = factors_ref[block * LANES : (block + 1) * LANES, :].T

    def rows_of(tile):
        return pl.ds(pl.multiple_of(tile * TILE, TILE), TILE)

    def part(tile, place):
        rows = pl.ds(pl.multiple_of(tile % here * TILE, TILE), TILE)
        return gathered_ref[tile // here, place, rows, :]

    def each(count, step):
        if count <= UNROLL:
            for index in range(count):
                step(index)
        else:

            def body(index, carry):
                step(index)
                return carry

            lax.fori_loop(0, count, body, 0)

    def normalize(tile, place, which):
        lane = lax.broadcasted_iota(jnp.int32, (TILE, LANES), 1)
        column = jnp.sum(
            jnp.where(lane == which % LANES, columns[which // LANES], 0.0), axis=1, keepdims=True
        )
        values = part(tile, place).astype(jnp.float32) * column * gains_ref[place : place + 1, :]
        return values.astype(jnp.bfloat16)

    def normalize_step(tile):
        normed_query[rows_of(tile), :] = normalize(tile, 0, tile)
        normed_key[rows_of(tile), :] = normalize(tile, 1, tile_count + tile)

    each(tile_count, normalize_step)
    for copy in to_smem:
        copy.wait()
    base = counts[tiles]

    def live_of(step):
        return [lists[step * most_live + slot] for slot in range(most_live)]

    def score_tile(place, step):
        keys = [normed_key[rows_of(live), :] for live in live_of(step)]
        score = lax.dot_general(
            normed_query[rows_of(base + step), :],
            jnp.concatenate(keys, axis=0),
            (((1,), (1,)), ((), ())),
            preferred_element_type=jnp.float32,
        )
        slot = lax.broadcasted_iota(jnp.int32, (1, most_live * TILE), 1) // TILE
        score = jnp.where(slot < counts[step], score, -jnp.inf)
        scores[place] = score
        largest = jnp.max(score, axis=1, keepdims=True)
        rows_kept[place] = jnp.broadcast_to(largest, (TILE, LANES))

    def weigh_tile(place, step):
        largest = jnp.concatenate([rows_kept[place]] * most_live, axis=1)
        weight = jnp.exp2((scores[place] - largest) * scale)
        weights[place] = weight.astype(jnp.bfloat16)
        denominators = jnp.sum(weight, axis=1, keepdims=True)
        rows_kept[place] = jnp.broadcast_to(denominators, (TILE, LANES))

    def value_tile(place, step):
        values = [part(live, 2) for live in live_of(step)]
        total = jnp.dot(
            weights[place], jnp.concatenate(values, axis=0), preferred_element_type=jnp.float32
        )
        out_ref[step] = (total / rows_kept[place]).astype(out_ref.dtype)

    def some_tiles(first):
        for turn in range(together + 2 * APART):
            for behind, stage in enumerate((score_tile, weigh_tile, value_tile)):
                place = turn - behind * APART
                if 0 <= place < together:
                    stage(place, first + place)

    if tiles == together:
        some_tiles(0)
    else:

        def several(index, carry):
            some_tiles(index * together)
            return carry

        lax.fori_loop(0, tiles // together, several, 0)


def attend(gathered, factors, gains, lists, counts, base, tiles):
    device_count, _, tokens_here, head_width = gathered.shape
    most_live = lists.shape[1]
    tile_count = device_count * tokens_here // TILE
    blocks = -(-factors.shape[0] // LANES)
    factors = jnp.pad(factors, ((0, blocks * LANES - factors.shape[0]), (0, 0)))
    lists = lists.reshape(-1)
    counts = jnp.concatenate([counts, base.reshape(1)])
    together = max(size for size in range(1, max(1, 64 // most_live) + 1) if tiles % size == 0)
    anywhere = pl.BlockSpec(memory_space=pl.ANY)
    vmem = pl.BlockSpec(memory_space=pltpu.VMEM)
    return pl.pallas_call(
        functools.partial(attend_kernel, most_live),
        out_shape=jax.ShapeDtypeStruct((tiles, TILE, head_width), jnp.bfloat16),
        in_specs=[anywhere] * 2 + [vmem] * 3,
        out_specs=vmem,
        scratch_shapes=[
            pltpu.SMEM(lists.shape, jnp.int32),
            pltpu.SMEM(counts.shape, jnp.int32),
            pltpu.VMEM((blocks, LANES, LANES), jnp.float32),
            pltpu.VMEM((tile_count * TILE, head_width), jnp.bfloat16),
            pltpu.VMEM((tile_count * TILE, head_width), jnp.bfloat16),
            pltpu.VMEM((together, TILE, most_live * TILE), jnp.float32),
            pltpu.VMEM((together, TILE, most_live * TILE), jnp.bfloat16),
            pltpu.VMEM((together, TILE, LANES), jnp.float32),
            pltpu.SemaphoreType.DMA((2,)),
        ],
        compiler_params=pltpu.CompilerParams(vmem_limit_bytes=48 * 1024 * 1024),
        name="attend",
    )(lists, counts, factors, gains, gathered)


def gather_over(values, axis):
    count = lax.axis_size(axis)
    if count & (count - 1):
        return lax.all_gather(values, axis)
    me = lax.axis_index(axis)
    held = values[None]
    reach = 1
    while reach < count:
        other = lax.ppermute(held, axis, [(i, i ^ reach) for i in range(count)])
        upper = (me & reach) != 0
        held = jnp.where(
            upper, jnp.concatenate([other, held], 0), jnp.concatenate([held, other], 0)
        )
        reach *= 2
    return held


def local(query_proj, key_proj, value_proj, query_gain, key_gain, live_tiles, live_count):
    tokens_here = query_proj.shape[0]
    heads_here = live_tiles.shape[0]
    head_width = query_proj.shape[1] // heads_here
    full_width = query_proj.shape[1] * lax.axis_size("tp")
    device_count = lax.axis_size("seq")
    group_size = device_count // heads_here
    my_index = lax.axis_index("seq")
    my_head = my_index // group_size
    my_member = my_index % group_size

    outgoing = pack(query_proj, key_proj, value_proj, heads_here)
    if group_size > 1:
        outgoing = jnp.repeat(outgoing, group_size, axis=0)
    gathered = lax.all_to_all(outgoing, "seq", split_axis=0, concat_axis=0, tiled=True)

    query_values = query_proj.astype(jnp.float32)
    key_values = key_proj.astype(jnp.float32)
    squares = jnp.stack(
        [jnp.sum(query_values * query_values, axis=1), jnp.sum(key_values * key_values, axis=1)]
    )
    squares = lax.psum(squares, "tp")
    factors = gather_over(lax.rsqrt(squares / full_width + epsilon), "seq")
    tile_count = device_count * tokens_here // TILE
    factors = factors.transpose(1, 0, 2).reshape(2 * tile_count, TILE)
    gains = jnp.stack([query_gain, key_gain]).reshape(2, heads_here, head_width)
    gains = lax.dynamic_index_in_dim(gains, my_head, 1, keepdims=False)

    per_member = tile_count // group_size
    base = my_member * per_member
    lists = lax.dynamic_index_in_dim(live_tiles, my_head, 0, keepdims=False)
    counts = lax.dynamic_index_in_dim(live_count, my_head, 0, keepdims=False)
    lists = lax.dynamic_slice_in_dim(lists, base, per_member, 0)
    counts = lax.dynamic_slice_in_dim(counts, base, per_member, 0)
    results = attend(
        gathered, factors, gains, lists, counts, base.astype(jnp.int32), per_member
    )
    if group_size > 1:
        placed = jnp.zeros((tile_count, TILE, head_width), jnp.bfloat16)
        results = lax.dynamic_update_slice_in_dim(placed, results, base, 0)
    results = results.reshape(device_count, tokens_here, head_width)
    returned = lax.all_to_all(results, "seq", split_axis=0, concat_axis=0, tiled=True)
    if group_size > 1:
        returned = returned.reshape(heads_here, group_size, tokens_here, head_width)
        returned = returned.astype(jnp.float32).sum(axis=1).astype(jnp.bfloat16)
    returned = returned.reshape(heads_here, tokens_here // 8, 8, head_width)
    return returned.transpose(1, 2, 0, 3).reshape(tokens_here, heads_here * head_width)


def solution(mesh):
    placed = (
        P("seq", "tp"),
        P("seq", "tp"),
        P("seq", "tp"),
        P("tp"),
        P("tp"),
        P("tp", None, None),
        P("tp", None),
    )
    return jax.shard_map(
        local, mesh=mesh, in_specs=placed, out_specs=P("seq", "tp"), check_vma=False
    )
```

```python
import functools
import math

import jax
import jax.numpy as jnp
from jax import lax
from jax.experimental import pallas as pl
from jax.experimental.pallas import tpu as pltpu
from jax.sharding import PartitionSpec as P

TILE = 128
LANES = 128
UNROLL = 16
APART = 4
epsilon = 1e-06


def pack_kernel(
    query_hbm, key_hbm, value_hbm, packed_hbm, query, key, value, packed, fetched, written
):
    heads, _, _, width = packed.shape
    pieces = written.shape[1]
    fields = ((query_hbm, query), (key_hbm, key), (value_hbm, value))
    fetches = [
        pltpu.make_async_copy(source, target, fetched.at[place])
        for place, (source, target) in enumerate(fields)
    ]
    for fetch in fetches:
        fetch.start()
    writes = []
    for place, (_, field) in enumerate(fields):
        fetches[place].wait()
        for piece in range(pieces):
            some = range(piece * heads // pieces, (piece + 1) * heads // pieces)
            for head in some:
                packed[head, place] = field[:, head * width : (head + 1) * width]
            span = pl.ds(some[0], len(some))
            writes.append(
                pltpu.make_async_copy(
                    packed.at[span, place], packed_hbm.at[span, place], written.at[place, piece]
                )
            )
            writes[-1].start()
    for write in writes:
        write.wait()


def pack(query, key, value, heads):
    tokens, columns = query.shape
    shape = (heads, 3, tokens, columns // heads)
    anywhere = pl.BlockSpec(memory_space=pl.ANY)
    return pl.pallas_call(
        pack_kernel,
        out_shape=jax.ShapeDtypeStruct(shape, query.dtype),
        in_specs=[anywhere] * 3,
        out_specs=anywhere,
        scratch_shapes=[pltpu.VMEM((tokens, columns), query.dtype)] * 3
        + [
            pltpu.VMEM(shape, query.dtype),
            pltpu.SemaphoreType.DMA((3,)),
            pltpu.SemaphoreType.DMA((3, 2 if heads % 2 == 0 else 1)),
        ],
        compiler_params=pltpu.CompilerParams(vmem_limit_bytes=56 * 1024 * 1024),
        name="pack_heads",
    )(query, key, value)


def attend_kernel(
    most_live,
    lists_hbm,
    counts_hbm,
    factors_ref,
    gains_ref,
    gathered_ref,
    out_ref,
    lists,
    counts,
    columns,
    normed_query,
    normed_key,
    scores,
    weights,
    rows_kept,
    sems,
):
    head_width = out_ref.shape[2]
    tiles = out_ref.shape[0]
    here = gathered_ref.shape[2] // TILE
    tile_count = gathered_ref.shape[0] * here
    together = scores.shape[0]
    scale = math.log2(math.e) / math.sqrt(head_width)
    to_smem = [
        pltpu.make_async_copy(lists_hbm, lists, sems.at[0]),
        pltpu.make_async_copy(counts_hbm, counts, sems.at[1]),
    ]
    for copy in to_smem:
        copy.start()
    for block in range(columns.shape[0]):
        columns[block] = factors_ref[block * LANES : (block + 1) * LANES, :].T

    def rows_of(tile):
        return pl.ds(pl.multiple_of(tile * TILE, TILE), TILE)

    def part(tile, place):
        rows = pl.ds(pl.multiple_of(tile % here * TILE, TILE), TILE)
        return gathered_ref[tile // here, place, rows, :]

    def each(count, step):
        if count <= UNROLL:
            for index in range(count):
                step(index)
        else:

            def body(index, carry):
                step(index)
                return carry

            lax.fori_loop(0, count, body, 0)

    def normalize(tile, place, which):
        lane = lax.broadcasted_iota(jnp.int32, (TILE, LANES), 1)
        column = jnp.sum(
            jnp.where(lane == which % LANES, columns[which // LANES], 0.0), axis=1, keepdims=True
        )
        values = part(tile, place).astype(jnp.float32) * column * gains_ref[place : place + 1, :]
        return values.astype(jnp.bfloat16)

    def normalize_step(tile):
        normed_query[rows_of(tile), :] = normalize(tile, 0, tile)
        normed_key[rows_of(tile), :] = normalize(tile, 1, tile_count + tile)

    each(tile_count, normalize_step)
    for copy in to_smem:
        copy.wait()
    base = counts[tiles]

    def live_of(step):
        return [lists[step * most_live + slot] for slot in range(most_live)]

    def score_tile(place, step):
        keys = [normed_key[rows_of(live), :] for live in live_of(step)]
        score = lax.dot_general(
            normed_query[rows_of(base + step), :],
            jnp.concatenate(keys, axis=0),
            (((1,), (1,)), ((), ())),
            preferred_element_type=jnp.float32,
        )
        slot = lax.broadcasted_iota(jnp.int32, (1, most_live * TILE), 1) // TILE
        score = jnp.where(slot < counts[step], score, -jnp.inf)
        scores[place] = score
        largest = jnp.max(score, axis=1, keepdims=True)
        rows_kept[place] = jnp.broadcast_to(largest, (TILE, LANES))

    def weigh_tile(place, step):
        largest = jnp.concatenate([rows_kept[place]] * most_live, axis=1)
        weight = jnp.exp2((scores[place] - largest) * scale)
        weights[place] = weight.astype(jnp.bfloat16)
        denominators = jnp.sum(weight, axis=1, keepdims=True)
        rows_kept[place] = jnp.broadcast_to(denominators, (TILE, LANES))

    def value_tile(place, step):
        values = [part(live, 2) for live in live_of(step)]
        total = jnp.dot(
            weights[place], jnp.concatenate(values, axis=0), preferred_element_type=jnp.float32
        )
        out_ref[step] = (total / rows_kept[place]).astype(out_ref.dtype)

    def some_tiles(first):
        for turn in range(together + 2 * APART):
            for behind, stage in enumerate((score_tile, weigh_tile, value_tile)):
                place = turn - behind * APART
                if 0 <= place < together:
                    stage(place, first + place)

    if tiles == together:
        some_tiles(0)
    else:

        def several(index, carry):
            some_tiles(index * together)
            return carry

        lax.fori_loop(0, tiles // together, several, 0)


def attend(gathered, factors, gains, lists, counts, base, tiles):
    device_count, _, tokens_here, head_width = gathered.shape
    most_live = lists.shape[1]
    tile_count = device_count * tokens_here // TILE
    blocks = -(-factors.shape[0] // LANES)
    factors = jnp.pad(factors, ((0, blocks * LANES - factors.shape[0]), (0, 0)))
    lists = lists.reshape(-1)
    counts = jnp.concatenate([counts, base.reshape(1)])
    together = max(size for size in range(1, max(1, 64 // most_live) + 1) if tiles % size == 0)
    anywhere = pl.BlockSpec(memory_space=pl.ANY)
    vmem = pl.BlockSpec(memory_space=pltpu.VMEM)
    return pl.pallas_call(
        functools.partial(attend_kernel, most_live),
        out_shape=jax.ShapeDtypeStruct((tiles, TILE, head_width), jnp.bfloat16),
        in_specs=[anywhere] * 2 + [vmem] * 3,
        out_specs=vmem,
        scratch_shapes=[
            pltpu.SMEM(lists.shape, jnp.int32),
            pltpu.SMEM(counts.shape, jnp.int32),
            pltpu.VMEM((blocks, LANES, LANES), jnp.float32),
            pltpu.VMEM((tile_count * TILE, head_width), jnp.bfloat16),
            pltpu.VMEM((tile_count * TILE, head_width), jnp.bfloat16),
            pltpu.VMEM((together, TILE, most_live * TILE), jnp.float32),
            pltpu.VMEM((together, TILE, most_live * TILE), jnp.bfloat16),
            pltpu.VMEM((together, TILE, LANES), jnp.float32),
            pltpu.SemaphoreType.DMA((2,)),
        ],
        compiler_params=pltpu.CompilerParams(vmem_limit_bytes=48 * 1024 * 1024),
        name="attend",
    )(lists, counts, factors, gains, gathered)


def squares_of(query, key):
    query, key = query.astype(jnp.float32), key.astype(jnp.float32)
    return jnp.stack([jnp.sum(query * query, axis=1), jnp.sum(key * key, axis=1)])


def swapped(held, reach, halves):
    count, width = lax.axis_size("seq"), lax.axis_size("tp")
    pairs = [(i * width + t, (i ^ reach) * width + t) for i in range(count) for t in halves]
    return lax.ppermute(held, ("seq", "tp"), pairs)


def doubled(held, reach, halves):
    other = swapped(held, reach, halves)
    upper = (lax.axis_index("seq") & reach) != 0
    first, second = jnp.where(upper, other, held), jnp.where(upper, held, other)
    return jnp.stack([first, second], axis=held.ndim - 2)


def local(query_proj, key_proj, value_proj, query_gain, key_gain, live_tiles, live_count):
    tokens_here = query_proj.shape[0]
    heads_here = live_tiles.shape[0]
    head_width = query_proj.shape[1] // heads_here
    full_width = query_proj.shape[1] * lax.axis_size("tp")
    device_count = lax.axis_size("seq")
    group_size = device_count // heads_here
    my_index = lax.axis_index("seq")
    my_head = my_index // group_size
    my_member = my_index % group_size

    outgoing = pack(query_proj, key_proj, value_proj, heads_here)
    halves = range(lax.axis_size("tp"))
    first_half = lax.axis_index("tp") == 0
    reaches = [1 << bit for bit in reversed(range((device_count - 1).bit_length()))]
    far, near = reaches[: len(reaches) // 2], reaches[len(reaches) // 2 :]
    spread = 1 << len(far)

    def gather_far(query, key):
        held = squares_of(query, key)
        for reach in far:
            held = doubled(held, reach, halves[:1])
        return held.reshape(spread, 2, tokens_here)

    def nothing(query, key):
        return jnp.zeros((spread, 2, tokens_here), jnp.float32)

    early = lax.cond(first_half, gather_far, nothing, query_proj, key_proj)
    outgoing, early = lax.optimization_barrier((outgoing, early))
    if group_size > 1:
        outgoing = jnp.repeat(outgoing, group_size, axis=0)
    gathered = lax.all_to_all(outgoing, "seq", split_axis=0, concat_axis=0, tiled=True)

    place = jnp.arange(spread)[:, None, None] == my_index // (device_count // spread)
    own = jnp.where(place, squares_of(query_proj, key_proj)[None], 0.0)
    held = jnp.where(first_half, early, own)
    for reach in near:
        held = doubled(held, reach, halves)
    for reach in reversed(far):
        held = held + swapped(held, reach, halves[1:])
    squares = lax.psum(held.reshape(device_count, 2, tokens_here), "tp")
    factors = lax.rsqrt(squares / full_width + epsilon)
    tile_count = device_count * tokens_here // TILE
    factors = factors.transpose(1, 0, 2).reshape(2 * tile_count, TILE)
    gains = jnp.stack([query_gain, key_gain]).reshape(2, heads_here, head_width)
    gains = lax.dynamic_index_in_dim(gains, my_head, 1, keepdims=False)

    per_member = tile_count // group_size
    base = my_member * per_member
    lists = lax.dynamic_index_in_dim(live_tiles, my_head, 0, keepdims=False)
    counts = lax.dynamic_index_in_dim(live_count, my_head, 0, keepdims=False)
    lists = lax.dynamic_slice_in_dim(lists, base, per_member, 0)
    counts = lax.dynamic_slice_in_dim(counts, base, per_member, 0)
    results = attend(
        gathered, factors, gains, lists, counts, base.astype(jnp.int32), per_member
    )
    if group_size > 1:
        placed = jnp.zeros((tile_count, TILE, head_width), jnp.bfloat16)
        results = lax.dynamic_update_slice_in_dim(placed, results, base, 0)
    results = results.reshape(device_count, tokens_here, head_width)
    returned = lax.all_to_all(results, "seq", split_axis=0, concat_axis=0, tiled=True)
    if group_size > 1:
        returned = returned.reshape(heads_here, group_size, tokens_here, head_width)
        returned = returned.astype(jnp.float32).sum(axis=1).astype(jnp.bfloat16)
    returned = returned.reshape(heads_here, tokens_here // 8, 8, head_width)
    return returned.transpose(1, 2, 0, 3).reshape(tokens_here, heads_here * head_width)


def solution(mesh):
    placed = (
        P("seq", "tp"),
        P("seq", "tp"),
        P("seq", "tp"),
        P("tp"),
        P("tp"),
        P("tp", None, None),
        P("tp", None),
    )
    return jax.shard_map(
        local, mesh=mesh, in_specs=placed, out_specs=P("seq", "tp"), check_vma=False
    )
```

```python
import functools
import math

import jax
import jax.numpy as jnp
from jax import lax
from jax.experimental import pallas as pl
from jax.experimental.pallas import tpu as pltpu
from jax.sharding import PartitionSpec as P

TILE = 128
LANES = 128
UNROLL = 16
APART = 4
epsilon = 1e-06


def pack_kernel(
    query_hbm, key_hbm, value_hbm, packed_hbm, query, key, value, packed, fetched, written
):
    heads, _, _, width = packed.shape
    pieces = written.shape[1]
    fields = ((query_hbm, query), (key_hbm, key), (value_hbm, value))
    fetches = [
        pltpu.make_async_copy(source, target, fetched.at[place])
        for place, (source, target) in enumerate(fields)
    ]
    for fetch in fetches:
        fetch.start()
    writes = []
    for place, (_, field) in enumerate(fields):
        fetches[place].wait()
        for piece in range(pieces):
            some = range(piece * heads // pieces, (piece + 1) * heads // pieces)
            for head in some:
                packed[head, place] = field[:, head * width : (head + 1) * width]
            span = pl.ds(some[0], len(some))
            writes.append(
                pltpu.make_async_copy(
                    packed.at[span, place], packed_hbm.at[span, place], written.at[place, piece]
                )
            )
            writes[-1].start()
    for write in writes:
        write.wait()


def pack(query, key, value, heads):
    tokens, columns = query.shape
    shape = (heads, 3, tokens, columns // heads)
    anywhere = pl.BlockSpec(memory_space=pl.ANY)
    return pl.pallas_call(
        pack_kernel,
        out_shape=jax.ShapeDtypeStruct(shape, query.dtype),
        in_specs=[anywhere] * 3,
        out_specs=anywhere,
        scratch_shapes=[pltpu.VMEM((tokens, columns), query.dtype)] * 3
        + [
            pltpu.VMEM(shape, query.dtype),
            pltpu.SemaphoreType.DMA((3,)),
            pltpu.SemaphoreType.DMA((3, 2 if heads % 2 == 0 else 1)),
        ],
        compiler_params=pltpu.CompilerParams(vmem_limit_bytes=56 * 1024 * 1024),
        name="pack_heads",
    )(query, key, value)


def attend_kernel(
    most_live,
    lists_hbm,
    counts_hbm,
    factors_ref,
    gains_ref,
    gathered_ref,
    out_ref,
    lists,
    counts,
    columns,
    normed_query,
    normed_key,
    scores,
    weights,
    rows_kept,
    sems,
):
    head_width = out_ref.shape[2]
    tiles = out_ref.shape[0]
    here = gathered_ref.shape[2] // TILE
    tile_count = gathered_ref.shape[0] * here
    together = scores.shape[0]
    scale = math.log2(math.e) / math.sqrt(head_width)
    to_smem = [
        pltpu.make_async_copy(lists_hbm, lists, sems.at[0]),
        pltpu.make_async_copy(counts_hbm, counts, sems.at[1]),
    ]
    for copy in to_smem:
        copy.start()
    for block in range(columns.shape[0]):
        columns[block] = factors_ref[block * LANES : (block + 1) * LANES, :].T

    def rows_of(tile):
        return pl.ds(pl.multiple_of(tile * TILE, TILE), TILE)

    def part(tile, place):
        rows = pl.ds(pl.multiple_of(tile % here * TILE, TILE), TILE)
        return gathered_ref[tile // here, place, rows, :]

    def each(count, step):
        if count <= UNROLL:
            for index in range(count):
                step(index)
        else:

            def body(index, carry):
                step(index)
                return carry

            lax.fori_loop(0, count, body, 0)

    def normalize(tile, place, which):
        lane = lax.broadcasted_iota(jnp.int32, (TILE, LANES), 1)
        column = jnp.sum(
            jnp.where(lane == which % LANES, columns[which // LANES], 0.0), axis=1, keepdims=True
        )
        values = part(tile, place).astype(jnp.float32) * column * gains_ref[place : place + 1, :]
        return values.astype(jnp.bfloat16)

    def normalize_step(tile):
        normed_query[rows_of(tile), :] = normalize(tile, 0, tile)
        normed_key[rows_of(tile), :] = normalize(tile, 1, tile_count + tile)

    each(tile_count, normalize_step)
    for copy in to_smem:
        copy.wait()
    base = counts[tiles]

    def live_of(step):
        return [lists[step * most_live + slot] for slot in range(most_live)]

    def score_tile(place, step):
        keys = [normed_key[rows_of(live), :] for live in live_of(step)]
        score = lax.dot_general(
            normed_query[rows_of(base + step), :],
            jnp.concatenate(keys, axis=0),
            (((1,), (1,)), ((), ())),
            preferred_element_type=jnp.float32,
        )
        slot = lax.broadcasted_iota(jnp.int32, (1, most_live * TILE), 1) // TILE
        score = jnp.where(slot < counts[step], score, -jnp.inf)
        scores[place] = score
        largest = jnp.max(score, axis=1, keepdims=True)
        rows_kept[place] = jnp.broadcast_to(largest, (TILE, LANES))

    def weigh_tile(place, step):
        largest = jnp.concatenate([rows_kept[place]] * most_live, axis=1)
        weight = jnp.exp2((scores[place] - largest) * scale)
        weights[place] = weight.astype(jnp.bfloat16)
        denominators = jnp.sum(weight, axis=1, keepdims=True)
        rows_kept[place] = jnp.broadcast_to(denominators, (TILE, LANES))

    def value_tile(place, step):
        values = [part(live, 2) for live in live_of(step)]
        total = jnp.dot(
            weights[place], jnp.concatenate(values, axis=0), preferred_element_type=jnp.float32
        )
        out_ref[step] = (total / rows_kept[place]).astype(out_ref.dtype)

    def some_tiles(first):
        for turn in range(together + 2 * APART):
            for behind, stage in enumerate((score_tile, weigh_tile, value_tile)):
                place = turn - behind * APART
                if 0 <= place < together:
                    stage(place, first + place)

    if tiles == together:
        some_tiles(0)
    else:

        def several(index, carry):
            some_tiles(index * together)
            return carry

        lax.fori_loop(0, tiles // together, several, 0)


def attend(gathered, factors, gains, lists, counts, base, tiles):
    device_count, _, tokens_here, head_width = gathered.shape
    most_live = lists.shape[1]
    tile_count = device_count * tokens_here // TILE
    blocks = -(-factors.shape[0] // LANES)
    factors = jnp.pad(factors, ((0, blocks * LANES - factors.shape[0]), (0, 0)))
    lists = lists.reshape(-1)
    counts = jnp.concatenate([counts, base.reshape(1)])
    together = max(size for size in range(1, max(1, 64 // most_live) + 1) if tiles % size == 0)
    anywhere = pl.BlockSpec(memory_space=pl.ANY)
    vmem = pl.BlockSpec(memory_space=pltpu.VMEM)
    return pl.pallas_call(
        functools.partial(attend_kernel, most_live),
        out_shape=jax.ShapeDtypeStruct((tiles, TILE, head_width), jnp.bfloat16),
        in_specs=[anywhere] * 2 + [vmem] * 3,
        out_specs=vmem,
        scratch_shapes=[
            pltpu.SMEM(lists.shape, jnp.int32),
            pltpu.SMEM(counts.shape, jnp.int32),
            pltpu.VMEM((blocks, LANES, LANES), jnp.float32),
            pltpu.VMEM((tile_count * TILE, head_width), jnp.bfloat16),
            pltpu.VMEM((tile_count * TILE, head_width), jnp.bfloat16),
            pltpu.VMEM((together, TILE, most_live * TILE), jnp.float32),
            pltpu.VMEM((together, TILE, most_live * TILE), jnp.bfloat16),
            pltpu.VMEM((together, TILE, LANES), jnp.float32),
            pltpu.SemaphoreType.DMA((2,)),
        ],
        compiler_params=pltpu.CompilerParams(vmem_limit_bytes=48 * 1024 * 1024),
        name="attend",
    )(lists, counts, factors, gains, gathered)


def squares_of(query, key):
    query, key = query.astype(jnp.float32), key.astype(jnp.float32)
    return jnp.stack([jnp.sum(query * query, axis=1), jnp.sum(key * key, axis=1)])


def swapped(held, reach, halves):
    count, width = lax.axis_size("seq"), lax.axis_size("tp")
    pairs = [(i * width + t, (i ^ reach) * width + t) for i in range(count) for t in halves]
    return lax.ppermute(held, ("seq", "tp"), pairs)


def doubled(held, reach, halves, across=None):
    other = swapped(held, across or reach, halves)
    upper = (lax.axis_index("seq") & reach) != 0
    first, second = jnp.where(upper, other, held), jnp.where(upper, held, other)
    return jnp.stack([first, second], axis=held.ndim - 2)


def local(query_proj, key_proj, value_proj, query_gain, key_gain, live_tiles, live_count):
    tokens_here = query_proj.shape[0]
    heads_here = live_tiles.shape[0]
    head_width = query_proj.shape[1] // heads_here
    full_width = query_proj.shape[1] * lax.axis_size("tp")
    device_count = lax.axis_size("seq")
    group_size = device_count // heads_here
    my_index = lax.axis_index("seq")
    my_head = my_index // group_size
    my_member = my_index % group_size

    outgoing = pack(query_proj, key_proj, value_proj, heads_here)
    halves = range(lax.axis_size("tp"))
    first_half = lax.axis_index("tp") == 0
    reaches = [1 << bit for bit in reversed(range((device_count - 1).bit_length()))]
    far, near = reaches[: len(reaches) // 2], reaches[len(reaches) // 2 :]
    spread = 1 << len(far)

    def gather_far(query, key):
        held = squares_of(query, key)
        for reach in far:
            held = doubled(held, reach, halves[:1], reach + sum(far[: far.index(reach)]))
        return held.reshape(spread, 2, tokens_here)

    def nothing(query, key):
        return jnp.zeros((spread, 2, tokens_here), jnp.float32)

    early = lax.cond(first_half, gather_far, nothing, query_proj, key_proj)
    outgoing, early = lax.optimization_barrier((outgoing, early))
    if group_size > 1:
        outgoing = jnp.repeat(outgoing, group_size, axis=0)
    gathered = lax.all_to_all(outgoing, "seq", split_axis=0, concat_axis=0, tiled=True)

    def rest_of_first(early, query, key):
        for reach in near:
            early = doubled(early, reach, halves[:1])
        return early.reshape(device_count, 2, tokens_here)

    def all_of_second(early, query, key):
        held = squares_of(query, key)
        for reach in near:
            held = doubled(held, reach, halves[1:])
        held = held.reshape(-1, 2, tokens_here)
        for reach in reversed(far):
            other = swapped(held, reach, halves[1:])
            upper = (my_index & reach) != 0
            held = jnp.concatenate(
                [jnp.where(upper, other, held), jnp.where(upper, held, other)], axis=0
            )
        return held

    held = lax.cond(first_half, rest_of_first, all_of_second, early, query_proj, key_proj)
    squares = lax.psum(held, "tp")
    factors = lax.rsqrt(squares / full_width + epsilon)
    tile_count = device_count * tokens_here // TILE
    factors = factors.transpose(1, 0, 2).reshape(2 * tile_count, TILE)
    gains = jnp.stack([query_gain, key_gain]).reshape(2, heads_here, head_width)
    gains = lax.dynamic_index_in_dim(gains, my_head, 1, keepdims=False)

    per_member = tile_count // group_size
    base = my_member * per_member
    lists = lax.dynamic_index_in_dim(live_tiles, my_head, 0, keepdims=False)
    counts = lax.dynamic_index_in_dim(live_count, my_head, 0, keepdims=False)
    lists = lax.dynamic_slice_in_dim(lists, base, per_member, 0)
    counts = lax.dynamic_slice_in_dim(counts, base, per_member, 0)
    results = attend(
        gathered, factors, gains, lists, counts, base.astype(jnp.int32), per_member
    )
    if group_size > 1:
        placed = jnp.zeros((tile_count, TILE, head_width), jnp.bfloat16)
        results = lax.dynamic_update_slice_in_dim(placed, results, base, 0)
    results = results.reshape(device_count, tokens_here, head_width)
    returned = lax.all_to_all(results, "seq", split_axis=0, concat_axis=0, tiled=True)
    if group_size > 1:
        returned = returned.reshape(heads_here, group_size, tokens_here, head_width)
        returned = returned.astype(jnp.float32).sum(axis=1).astype(jnp.bfloat16)
    returned = returned.reshape(heads_here, tokens_here // 8, 8, head_width)
    return returned.transpose(1, 2, 0, 3).reshape(tokens_here, heads_here * head_width)


def solution(mesh):
    placed = (
        P("seq", "tp"),
        P("seq", "tp"),
        P("seq", "tp"),
        P("tp"),
        P("tp"),
        P("tp", None, None),
        P("tp", None),
    )
    return jax.shard_map(
        local, mesh=mesh, in_specs=placed, out_specs=P("seq", "tp"), check_vma=False
    )
```

```python
import functools
import math

import jax
import jax.numpy as jnp
from jax import lax
from jax.experimental import pallas as pl
from jax.experimental.pallas import tpu as pltpu
from jax.sharding import PartitionSpec as P

TILE = 128
LANES = 128
UNROLL = 16
APART = 4
epsilon = 1e-06


def pack_kernel(
    query_hbm, key_hbm, value_hbm, packed_hbm, query, key, value, packed, fetched, written
):
    heads, _, _, width = packed.shape
    pieces = written.shape[1]
    fields = ((query_hbm, query), (key_hbm, key), (value_hbm, value))
    fetches = [
        pltpu.make_async_copy(source, target, fetched.at[place])
        for place, (source, target) in enumerate(fields)
    ]
    for fetch in fetches:
        fetch.start()
    writes = []
    for place, (_, field) in enumerate(fields):
        fetches[place].wait()
        for piece in range(pieces):
            some = range(piece * heads // pieces, (piece + 1) * heads // pieces)
            for head in some:
                packed[head, place] = field[:, head * width : (head + 1) * width]
            span = pl.ds(some[0], len(some))
            writes.append(
                pltpu.make_async_copy(
                    packed.at[span, place], packed_hbm.at[span, place], written.at[place, piece]
                )
            )
            writes[-1].start()
    for write in writes:
        write.wait()


def pack(query, key, value, heads):
    tokens, columns = query.shape
    shape = (heads, 3, tokens, columns // heads)
    anywhere = pl.BlockSpec(memory_space=pl.ANY)
    return pl.pallas_call(
        pack_kernel,
        out_shape=jax.ShapeDtypeStruct(shape, query.dtype),
        in_specs=[anywhere] * 3,
        out_specs=anywhere,
        scratch_shapes=[pltpu.VMEM((tokens, columns), query.dtype)] * 3
        + [
            pltpu.VMEM(shape, query.dtype),
            pltpu.SemaphoreType.DMA((3,)),
            pltpu.SemaphoreType.DMA((3, 2 if heads % 2 == 0 else 1)),
        ],
        compiler_params=pltpu.CompilerParams(vmem_limit_bytes=56 * 1024 * 1024),
        name="pack_heads",
    )(query, key, value)


def attend_kernel(
    most_live,
    lists_hbm,
    counts_hbm,
    factors_ref,
    gains_ref,
    gathered_ref,
    out_ref,
    lists,
    counts,
    columns,
    normed_query,
    normed_key,
    scores,
    weights,
    rows_kept,
    sems,
):
    head_width = out_ref.shape[2]
    tiles = out_ref.shape[0]
    here = gathered_ref.shape[2] // TILE
    tile_count = gathered_ref.shape[0] * here
    together = scores.shape[0]
    scale = math.log2(math.e) / math.sqrt(head_width)
    to_smem = [
        pltpu.make_async_copy(lists_hbm, lists, sems.at[0]),
        pltpu.make_async_copy(counts_hbm, counts, sems.at[1]),
    ]
    for copy in to_smem:
        copy.start()
    for block in range(columns.shape[0]):
        columns[block] = factors_ref[block * LANES : (block + 1) * LANES, :].T

    def rows_of(tile):
        return pl.ds(pl.multiple_of(tile * TILE, TILE), TILE)

    def part(tile, place):
        rows = pl.ds(pl.multiple_of(tile % here * TILE, TILE), TILE)
        return gathered_ref[tile // here, place, rows, :]

    def each(count, step):
        if count <= UNROLL:
            for index in range(count):
                step(index)
        else:

            def body(index, carry):
                step(index)
                return carry

            lax.fori_loop(0, count, body, 0)

    def normalize(tile, place, which):
        lane = lax.broadcasted_iota(jnp.int32, (TILE, LANES), 1)
        column = jnp.sum(
            jnp.where(lane == which % LANES, columns[which // LANES], 0.0), axis=1, keepdims=True
        )
        values = part(tile, place).astype(jnp.float32) * column * gains_ref[place : place + 1, :]
        return values.astype(jnp.bfloat16)

    def normalize_step(tile):
        normed_query[rows_of(tile), :] = normalize(tile, 0, tile)
        normed_key[rows_of(tile), :] = normalize(tile, 1, tile_count + tile)

    each(tile_count, normalize_step)
    for copy in to_smem:
        copy.wait()
    base = counts[tiles]

    def live_of(step):
        return [lists[step * most_live + slot] for slot in range(most_live)]

    def score_tile(place, step):
        keys = [normed_key[rows_of(live), :] for live in live_of(step)]
        score = lax.dot_general(
            normed_query[rows_of(base + step), :],
            jnp.concatenate(keys, axis=0),
            (((1,), (1,)), ((), ())),
            preferred_element_type=jnp.float32,
        )
        slot = lax.broadcasted_iota(jnp.int32, (1, most_live * TILE), 1) // TILE
        score = jnp.where(slot < counts[step], score, -jnp.inf)
        scores[place] = score
        largest = jnp.max(score, axis=1, keepdims=True)
        rows_kept[place] = jnp.broadcast_to(largest, (TILE, LANES))

    def weigh_tile(place, step):
        largest = jnp.concatenate([rows_kept[place]] * most_live, axis=1)
        weight = jnp.exp2((scores[place] - largest) * scale)
        weights[place] = weight.astype(jnp.bfloat16)
        denominators = jnp.sum(weight, axis=1, keepdims=True)
        rows_kept[place] = jnp.broadcast_to(denominators, (TILE, LANES))

    def value_tile(place, step):
        values = [part(live, 2) for live in live_of(step)]
        total = jnp.dot(
            weights[place], jnp.concatenate(values, axis=0), preferred_element_type=jnp.float32
        )
        out_ref[step] = (total / rows_kept[place]).astype(out_ref.dtype)

    def some_tiles(first):
        for turn in range(together + 2 * APART):
            for behind, stage in enumerate((score_tile, weigh_tile, value_tile)):
                place = turn - behind * APART
                if 0 <= place < together:
                    stage(place, first + place)

    if tiles == together:
        some_tiles(0)
    else:

        def several(index, carry):
            some_tiles(index * together)
            return carry

        lax.fori_loop(0, tiles // together, several, 0)


def attend(gathered, factors, gains, lists, counts, base, tiles):
    device_count, _, tokens_here, head_width = gathered.shape
    most_live = lists.shape[1]
    tile_count = device_count * tokens_here // TILE
    blocks = -(-factors.shape[0] // LANES)
    factors = jnp.pad(factors, ((0, blocks * LANES - factors.shape[0]), (0, 0)))
    lists = lists.reshape(-1)
    counts = jnp.concatenate([counts, base.reshape(1)])
    together = max(size for size in range(1, max(1, 64 // most_live) + 1) if tiles % size == 0)
    anywhere = pl.BlockSpec(memory_space=pl.ANY)
    vmem = pl.BlockSpec(memory_space=pltpu.VMEM)
    return pl.pallas_call(
        functools.partial(attend_kernel, most_live),
        out_shape=jax.ShapeDtypeStruct((tiles, TILE, head_width), jnp.bfloat16),
        in_specs=[anywhere] * 2 + [vmem] * 3,
        out_specs=vmem,
        scratch_shapes=[
            pltpu.SMEM(lists.shape, jnp.int32),
            pltpu.SMEM(counts.shape, jnp.int32),
            pltpu.VMEM((blocks, LANES, LANES), jnp.float32),
            pltpu.VMEM((tile_count * TILE, head_width), jnp.bfloat16),
            pltpu.VMEM((tile_count * TILE, head_width), jnp.bfloat16),
            pltpu.VMEM((together, TILE, most_live * TILE), jnp.float32),
            pltpu.VMEM((together, TILE, most_live * TILE), jnp.bfloat16),
            pltpu.VMEM((together, TILE, LANES), jnp.float32),
            pltpu.SemaphoreType.DMA((2,)),
        ],
        compiler_params=pltpu.CompilerParams(vmem_limit_bytes=48 * 1024 * 1024),
        name="attend",
    )(lists, counts, factors, gains, gathered)


def squares_of(query, key):
    query, key = query.astype(jnp.float32), key.astype(jnp.float32)
    return jnp.stack([jnp.sum(query * query, axis=1), jnp.sum(key * key, axis=1)])


def swapped(held, reach, halves):
    count, width = lax.axis_size("seq"), lax.axis_size("tp")
    pairs = [(i * width + t, (i ^ reach) * width + t) for i in range(count) for t in halves]
    return lax.ppermute(held, ("seq", "tp"), pairs)


def doubled(held, reach, halves, across=None):
    other = swapped(held, across or reach, halves)
    upper = (lax.axis_index("seq") & reach) != 0
    first, second = jnp.where(upper, other, held), jnp.where(upper, held, other)
    return jnp.stack([first, second], axis=held.ndim - 2)


def local(query_proj, key_proj, value_proj, query_gain, key_gain, live_tiles, live_count):
    tokens_here = query_proj.shape[0]
    heads_here = live_tiles.shape[0]
    head_width = query_proj.shape[1] // heads_here
    full_width = query_proj.shape[1] * lax.axis_size("tp")
    device_count = lax.axis_size("seq")
    group_size = device_count // heads_here
    my_index = lax.axis_index("seq")
    my_head = my_index // group_size
    my_member = my_index % group_size

    outgoing = pack(query_proj, key_proj, value_proj, heads_here)
    halves = range(lax.axis_size("tp"))
    first_half = lax.axis_index("tp") == 0
    reaches = [1 << bit for bit in reversed(range((device_count - 1).bit_length()))]
    far, near = reaches[: len(reaches) // 2], reaches[len(reaches) // 2 :]
    spread = 1 << len(far)

    def gather_far(query, key):
        held = squares_of(query, key)
        for reach in far:
            held = doubled(held, reach, halves[:1], reach + sum(far[: far.index(reach)]))
        return held.reshape(spread, 2, tokens_here)

    def nothing(query, key):
        return jnp.zeros((spread, 2, tokens_here), jnp.float32)

    early = lax.cond(first_half, gather_far, nothing, query_proj, key_proj)
    outgoing, early = lax.optimization_barrier((outgoing, early))
    if group_size > 1:
        outgoing = jnp.repeat(outgoing, group_size, axis=0)
    gathered = lax.all_to_all(outgoing, "seq", split_axis=0, concat_axis=0, tiled=True)

    def rest_of_first(early, query, key):
        for reach in near:
            early = doubled(early, reach, halves[:1])
        return early.reshape(device_count, 2, tokens_here)

    def all_of_second(early, query, key):
        held = squares_of(query, key)
        for reach in near:
            held = doubled(held, reach, halves[1:])
        held = held.reshape(-1, 2, tokens_here)
        for reach in reversed(far):
            other = swapped(held, reach, halves[1:])
            upper = (my_index & reach) != 0
            held = jnp.concatenate(
                [jnp.where(upper, other, held), jnp.where(upper, held, other)], axis=0
            )
        return held

    held = lax.cond(first_half, rest_of_first, all_of_second, early, query_proj, key_proj)
    squares = held + lax.ppermute(held, "tp", [(0, 1), (1, 0)])
    factors = lax.rsqrt(squares / full_width + epsilon)
    tile_count = device_count * tokens_here // TILE
    factors = factors.transpose(1, 0, 2).reshape(2 * tile_count, TILE)
    gains = jnp.stack([query_gain, key_gain]).reshape(2, heads_here, head_width)
    gains = lax.dynamic_index_in_dim(gains, my_head, 1, keepdims=False)

    per_member = tile_count // group_size
    base = my_member * per_member
    lists = lax.dynamic_index_in_dim(live_tiles, my_head, 0, keepdims=False)
    counts = lax.dynamic_index_in_dim(live_count, my_head, 0, keepdims=False)
    lists = lax.dynamic_slice_in_dim(lists, base, per_member, 0)
    counts = lax.dynamic_slice_in_dim(counts, base, per_member, 0)
    results = attend(
        gathered, factors, gains, lists, counts, base.astype(jnp.int32), per_member
    )
    if group_size > 1:
        placed = jnp.zeros((tile_count, TILE, head_width), jnp.bfloat16)
        results = lax.dynamic_update_slice_in_dim(placed, results, base, 0)
    results = results.reshape(device_count, tokens_here, head_width)
    returned = lax.all_to_all(results, "seq", split_axis=0, concat_axis=0, tiled=True)
    if group_size > 1:
        returned = returned.reshape(heads_here, group_size, tokens_here, head_width)
        returned = returned.astype(jnp.float32).sum(axis=1).astype(jnp.bfloat16)
    returned = returned.reshape(heads_here, tokens_here // 8, 8, head_width)
    return returned.transpose(1, 2, 0, 3).reshape(tokens_here, heads_here * head_width)


def solution(mesh):
    placed = (
        P("seq", "tp"),
        P("seq", "tp"),
        P("seq", "tp"),
        P("tp"),
        P("tp"),
        P("tp", None, None),
        P("tp", None),
    )
    return jax.shard_map(
        local, mesh=mesh, in_specs=placed, out_specs=P("seq", "tp"), check_vma=False
    )
```

```python
import functools
import math

import jax
import jax.numpy as jnp
from jax import lax
from jax.experimental import pallas as pl
from jax.experimental.pallas import tpu as pltpu
from jax.sharding import PartitionSpec as P

TILE = 128
LANES = 128
UNROLL = 16
APART = 4
epsilon = 1e-06


def pack_kernel(
    query_hbm, key_hbm, value_hbm, packed_hbm, query, key, value, packed, fetched, written
):
    heads, _, _, width = packed.shape
    pieces = written.shape[1]
    fields = ((query_hbm, query), (key_hbm, key), (value_hbm, value))
    fetches = [
        pltpu.make_async_copy(source, target, fetched.at[place])
        for place, (source, target) in enumerate(fields)
    ]
    for fetch in fetches:
        fetch.start()
    writes = []
    for place, (_, field) in enumerate(fields):
        fetches[place].wait()
        for piece in range(pieces):
            some = range(piece * heads // pieces, (piece + 1) * heads // pieces)
            for head in some:
                packed[head, place] = field[:, head * width : (head + 1) * width]
            span = pl.ds(some[0], len(some))
            writes.append(
                pltpu.make_async_copy(
                    packed.at[span, place], packed_hbm.at[span, place], written.at[place, piece]
                )
            )
            writes[-1].start()
    for write in writes:
        write.wait()


def pack(query, key, value, heads):
    tokens, columns = query.shape
    shape = (heads, 3, tokens, columns // heads)
    anywhere = pl.BlockSpec(memory_space=pl.ANY)
    return pl.pallas_call(
        pack_kernel,
        out_shape=jax.ShapeDtypeStruct(shape, query.dtype),
        in_specs=[anywhere] * 3,
        out_specs=anywhere,
        scratch_shapes=[pltpu.VMEM((tokens, columns), query.dtype)] * 3
        + [
            pltpu.VMEM(shape, query.dtype),
            pltpu.SemaphoreType.DMA((3,)),
            pltpu.SemaphoreType.DMA((3, 2 if heads % 2 == 0 else 1)),
        ],
        compiler_params=pltpu.CompilerParams(vmem_limit_bytes=56 * 1024 * 1024),
        name="pack_heads",
    )(query, key, value)


def attend_kernel(
    most_live,
    lists_hbm,
    counts_hbm,
    factors_ref,
    gains_ref,
    gathered_ref,
    out_ref,
    lists,
    counts,
    columns,
    normed_query,
    normed_key,
    scores,
    weights,
    rows_kept,
    sems,
):
    head_width = out_ref.shape[2]
    tiles = out_ref.shape[0]
    here = gathered_ref.shape[2] // TILE
    tile_count = gathered_ref.shape[0] * here
    together = scores.shape[0]
    scale = math.log2(math.e) / math.sqrt(head_width)
    to_smem = [
        pltpu.make_async_copy(lists_hbm, lists, sems.at[0]),
        pltpu.make_async_copy(counts_hbm, counts, sems.at[1]),
    ]
    for copy in to_smem:
        copy.start()
    for block in range(columns.shape[0]):
        columns[block] = factors_ref[block * LANES : (block + 1) * LANES, :].T

    def rows_of(tile):
        return pl.ds(pl.multiple_of(tile * TILE, TILE), TILE)

    def part(tile, place):
        rows = pl.ds(pl.multiple_of(tile % here * TILE, TILE), TILE)
        return gathered_ref[tile // here, place, rows, :]

    def each(count, step):
        if count <= UNROLL:
            for index in range(count):
                step(index)
        else:

            def body(index, carry):
                step(index)
                return carry

            lax.fori_loop(0, count, body, 0)

    def normalize(tile, place, which):
        lane = lax.broadcasted_iota(jnp.int32, (TILE, LANES), 1)
        column = jnp.sum(
            jnp.where(lane == which % LANES, columns[which // LANES], 0.0), axis=1, keepdims=True
        )
        values = part(tile, place).astype(jnp.float32) * column * gains_ref[place : place + 1, :]
        return values.astype(jnp.bfloat16)

    def normalize_step(tile):
        normed_query[rows_of(tile), :] = normalize(tile, 0, tile)
        normed_key[rows_of(tile), :] = normalize(tile, 1, tile_count + tile)

    each(tile_count, normalize_step)
    for copy in to_smem:
        copy.wait()
    base = counts[tiles]

    def live_of(step):
        return [lists[step * most_live + slot] for slot in range(most_live)]

    def score_tile(place, step):
        keys = [normed_key[rows_of(live), :] for live in live_of(step)]
        score = lax.dot_general(
            normed_query[rows_of(base + step), :],
            jnp.concatenate(keys, axis=0),
            (((1,), (1,)), ((), ())),
            preferred_element_type=jnp.float32,
        )
        slots = [score[:, slot * TILE : (slot + 1) * TILE] for slot in range(most_live)]
        for slot in range(1, most_live):
            slots[slot] = jnp.where(slot < counts[step], slots[slot], -jnp.inf)
        score = jnp.concatenate(slots, axis=1)
        scores[place] = score
        largest = jnp.max(score, axis=1, keepdims=True)
        rows_kept[place] = jnp.broadcast_to(largest, (TILE, LANES))

    def weigh_tile(place, step):
        largest = jnp.concatenate([rows_kept[place]] * most_live, axis=1)
        weight = jnp.exp2((scores[place] - largest) * scale)
        weights[place] = weight.astype(jnp.bfloat16)
        denominators = jnp.sum(weight, axis=1, keepdims=True)
        rows_kept[place] = jnp.broadcast_to(denominators, (TILE, LANES))

    def value_tile(place, step):
        values = [part(live, 2) for live in live_of(step)]
        total = jnp.dot(
            weights[place], jnp.concatenate(values, axis=0), preferred_element_type=jnp.float32
        )
        out_ref[step] = (total / rows_kept[place]).astype(out_ref.dtype)

    def some_tiles(first):
        for turn in range(together + 2 * APART):
            for behind, stage in enumerate((score_tile, weigh_tile, value_tile)):
                place = turn - behind * APART
                if 0 <= place < together:
                    stage(place, first + place)

    if tiles == together:
        some_tiles(0)
    else:

        def several(index, carry):
            some_tiles(index * together)
            return carry

        lax.fori_loop(0, tiles // together, several, 0)


def attend(gathered, factors, gains, lists, counts, base, tiles):
    device_count, _, tokens_here, head_width = gathered.shape
    most_live = lists.shape[1]
    tile_count = device_count * tokens_here // TILE
    blocks = -(-factors.shape[0] // LANES)
    factors = jnp.pad(factors, ((0, blocks * LANES - factors.shape[0]), (0, 0)))
    lists = lists.reshape(-1)
    counts = jnp.concatenate([counts, base.reshape(1)])
    together = max(size for size in range(1, max(1, 64 // most_live) + 1) if tiles % size == 0)
    anywhere = pl.BlockSpec(memory_space=pl.ANY)
    vmem = pl.BlockSpec(memory_space=pltpu.VMEM)
    return pl.pallas_call(
        functools.partial(attend_kernel, most_live),
        out_shape=jax.ShapeDtypeStruct((tiles, TILE, head_width), jnp.bfloat16),
        in_specs=[anywhere] * 2 + [vmem] * 3,
        out_specs=vmem,
        scratch_shapes=[
            pltpu.SMEM(lists.shape, jnp.int32),
            pltpu.SMEM(counts.shape, jnp.int32),
            pltpu.VMEM((blocks, LANES, LANES), jnp.float32),
            pltpu.VMEM((tile_count * TILE, head_width), jnp.bfloat16),
            pltpu.VMEM((tile_count * TILE, head_width), jnp.bfloat16),
            pltpu.VMEM((together, TILE, most_live * TILE), jnp.float32),
            pltpu.VMEM((together, TILE, most_live * TILE), jnp.bfloat16),
            pltpu.VMEM((together, TILE, LANES), jnp.float32),
            pltpu.SemaphoreType.DMA((2,)),
        ],
        compiler_params=pltpu.CompilerParams(vmem_limit_bytes=48 * 1024 * 1024),
        name="attend",
    )(lists, counts, factors, gains, gathered)


def squares_of(query, key):
    query, key = query.astype(jnp.float32), key.astype(jnp.float32)
    return jnp.stack([jnp.sum(query * query, axis=1), jnp.sum(key * key, axis=1)])


def swapped(held, reach, halves):
    count, width = lax.axis_size("seq"), lax.axis_size("tp")
    pairs = [(i * width + t, (i ^ reach) * width + t) for i in range(count) for t in halves]
    return lax.ppermute(held, ("seq", "tp"), pairs)


def doubled(held, reach, halves, across=None):
    other = swapped(held, across or reach, halves)
    upper = (lax.axis_index("seq") & reach) != 0
    first, second = jnp.where(upper, other, held), jnp.where(upper, held, other)
    return jnp.stack([first, second], axis=held.ndim - 2)


def local(query_proj, key_proj, value_proj, query_gain, key_gain, live_tiles, live_count):
    tokens_here = query_proj.shape[0]
    heads_here = live_tiles.shape[0]
    head_width = query_proj.shape[1] // heads_here
    full_width = query_proj.shape[1] * lax.axis_size("tp")
    device_count = lax.axis_size("seq")
    group_size = device_count // heads_here
    my_index = lax.axis_index("seq")
    my_head = my_index // group_size
    my_member = my_index % group_size

    outgoing = pack(query_proj, key_proj, value_proj, heads_here)
    halves = range(lax.axis_size("tp"))
    first_half = lax.axis_index("tp") == 0
    reaches = [1 << bit for bit in reversed(range((device_count - 1).bit_length()))]
    far, near = reaches[: len(reaches) // 2], reaches[len(reaches) // 2 :]
    spread = 1 << len(far)

    def gather_far(query, key):
        held = squares_of(query, key)
        for reach in far:
            held = doubled(held, reach, halves[:1], reach + sum(far[: far.index(reach)]))
        return held.reshape(spread, 2, tokens_here)

    def nothing(query, key):
        return jnp.zeros((spread, 2, tokens_here), jnp.float32)

    early = lax.cond(first_half, gather_far, nothing, query_proj, key_proj)
    outgoing, early = lax.optimization_barrier((outgoing, early))
    if group_size > 1:
        outgoing = jnp.repeat(outgoing, group_size, axis=0)
    gathered = lax.all_to_all(outgoing, "seq", split_axis=0, concat_axis=0, tiled=True)

    def rest_of_first(early, query, key):
        for reach in near:
            early = doubled(early, reach, halves[:1])
        return early.reshape(device_count, 2, tokens_here)

    def all_of_second(early, query, key):
        held = squares_of(query, key)
        for reach in near:
            held = doubled(held, reach, halves[1:])
        held = held.reshape(-1, 2, tokens_here)
        for reach in reversed(far):
            other = swapped(held, reach, halves[1:])
            upper = (my_index & reach) != 0
            held = jnp.concatenate(
                [jnp.where(upper, other, held), jnp.where(upper, held, other)], axis=0
            )
        return held

    held = lax.cond(first_half, rest_of_first, all_of_second, early, query_proj, key_proj)
    squares = held + lax.ppermute(held, "tp", [(0, 1), (1, 0)])
    factors = lax.rsqrt(squares / full_width + epsilon)
    tile_count = device_count * tokens_here // TILE
    factors = factors.transpose(1, 0, 2).reshape(2 * tile_count, TILE)
    gains = jnp.stack([query_gain, key_gain]).reshape(2, heads_here, head_width)
    gains = lax.dynamic_index_in_dim(gains, my_head, 1, keepdims=False)

    per_member = tile_count // group_size
    base = my_member * per_member
    lists = lax.dynamic_index_in_dim(live_tiles, my_head, 0, keepdims=False)
    counts = lax.dynamic_index_in_dim(live_count, my_head, 0, keepdims=False)
    lists = lax.dynamic_slice_in_dim(lists, base, per_member, 0)
    counts = lax.dynamic_slice_in_dim(counts, base, per_member, 0)
    results = attend(
        gathered, factors, gains, lists, counts, base.astype(jnp.int32), per_member
    )
    if group_size > 1:
        placed = jnp.zeros((tile_count, TILE, head_width), jnp.bfloat16)
        results = lax.dynamic_update_slice_in_dim(placed, results, base, 0)
    results = results.reshape(device_count, tokens_here, head_width)
    returned = lax.all_to_all(results, "seq", split_axis=0, concat_axis=0, tiled=True)
    if group_size > 1:
        returned = returned.reshape(heads_here, group_size, tokens_here, head_width)
        returned = returned.astype(jnp.float32).sum(axis=1).astype(jnp.bfloat16)
    returned = returned.reshape(heads_here, tokens_here // 8, 8, head_width)
    return returned.transpose(1, 2, 0, 3).reshape(tokens_here, heads_here * head_width)


def solution(mesh):
    placed = (
        P("seq", "tp"),
        P("seq", "tp"),
        P("seq", "tp"),
        P("tp"),
        P("tp"),
        P("tp", None, None),
        P("tp", None),
    )
    return jax.shard_map(
        local, mesh=mesh, in_specs=placed, out_specs=P("seq", "tp"), check_vma=False
    )
```

```python
import functools
import math

import jax
import jax.numpy as jnp
from jax import lax
from jax.experimental import pallas as pl
from jax.experimental.pallas import tpu as pltpu
from jax.sharding import PartitionSpec as P

TILE = 128
LANES = 128
UNROLL = 16
APART = 4
epsilon = 1e-06


def pack_kernel(
    query_hbm, key_hbm, value_hbm, packed_hbm, query, key, value, packed, fetched, written
):
    heads, _, _, width = packed.shape
    pieces = written.shape[1]
    fields = ((query_hbm, query), (key_hbm, key), (value_hbm, value))
    fetches = [
        pltpu.make_async_copy(source, target, fetched.at[place])
        for place, (source, target) in enumerate(fields)
    ]
    for fetch in fetches:
        fetch.start()
    writes = []
    for place, (_, field) in enumerate(fields):
        fetches[place].wait()
        for piece in range(pieces):
            some = range(piece * heads // pieces, (piece + 1) * heads // pieces)
            for head in some:
                packed[head, place] = field[:, head * width : (head + 1) * width]
            span = pl.ds(some[0], len(some))
            writes.append(
                pltpu.make_async_copy(
                    packed.at[span, place], packed_hbm.at[span, place], written.at[place, piece]
                )
            )
            writes[-1].start()
    for write in writes:
        write.wait()


def pack(query, key, value, heads):
    tokens, columns = query.shape
    shape = (heads, 3, tokens, columns // heads)
    anywhere = pl.BlockSpec(memory_space=pl.ANY)
    return pl.pallas_call(
        pack_kernel,
        out_shape=jax.ShapeDtypeStruct(shape, query.dtype),
        in_specs=[anywhere] * 3,
        out_specs=anywhere,
        scratch_shapes=[pltpu.VMEM((tokens, columns), query.dtype)] * 3
        + [
            pltpu.VMEM(shape, query.dtype),
            pltpu.SemaphoreType.DMA((3,)),
            pltpu.SemaphoreType.DMA((3, 2 if heads % 2 == 0 else 1)),
        ],
        compiler_params=pltpu.CompilerParams(vmem_limit_bytes=56 * 1024 * 1024),
        name="pack_heads",
    )(query, key, value)


def attend_kernel(
    most_live,
    lists_hbm,
    counts_hbm,
    factors_ref,
    gains_ref,
    gathered_ref,
    out_ref,
    lists,
    counts,
    columns,
    normed_query,
    normed_key,
    scores,
    weights,
    rows_kept,
    sems,
):
    head_width = out_ref.shape[2]
    tiles = out_ref.shape[0]
    here = gathered_ref.shape[2] // TILE
    tile_count = gathered_ref.shape[0] * here
    together = scores.shape[0]
    scale = math.log2(math.e) / math.sqrt(head_width)
    to_smem = [
        pltpu.make_async_copy(lists_hbm, lists, sems.at[0]),
        pltpu.make_async_copy(counts_hbm, counts, sems.at[1]),
    ]
    for copy in to_smem:
        copy.start()
    for block in range(columns.shape[0]):
        columns[block] = factors_ref[block * LANES : (block + 1) * LANES, :].T

    def rows_of(tile):
        return pl.ds(pl.multiple_of(tile * TILE, TILE), TILE)

    def part(tile, place):
        rows = pl.ds(pl.multiple_of(tile % here * TILE, TILE), TILE)
        return gathered_ref[tile // here, place, rows, :]

    def each(count, step):
        if count <= UNROLL:
            for index in range(count):
                step(index)
        else:

            def body(index, carry):
                step(index)
                return carry

            lax.fori_loop(0, count, body, 0)

    def normalize(tile, place, which):
        lane = lax.broadcasted_iota(jnp.int32, (TILE, LANES), 1)
        column = jnp.sum(
            jnp.where(lane == which % LANES, columns[which // LANES], 0.0), axis=1, keepdims=True
        )
        values = part(tile, place).astype(jnp.float32) * column * gains_ref[place : place + 1, :]
        return values.astype(jnp.bfloat16)

    def normalize_step(tile):
        normed_query[rows_of(tile), :] = normalize(tile, 0, tile)
        normed_key[rows_of(tile), :] = normalize(tile, 1, tile_count + tile)

    each(tile_count, normalize_step)
    for copy in to_smem:
        copy.wait()
    base = counts[tiles]

    def live_of(step):
        return [lists[step * most_live + slot] for slot in range(most_live)]

    def score_tile(place, step):
        keys = [normed_key[rows_of(live), :] for live in live_of(step)]
        score = lax.dot_general(
            normed_query[rows_of(base + step), :],
            jnp.concatenate(keys, axis=0),
            (((1,), (1,)), ((), ())),
            preferred_element_type=jnp.float32,
        )
        slots = [score[:, slot * TILE : (slot + 1) * TILE] for slot in range(most_live)]
        for slot in range(1, most_live):
            slots[slot] = jnp.where(slot < counts[step], slots[slot], -jnp.inf)
        score = jnp.concatenate(slots, axis=1)
        scores[place] = score
        largest = jnp.max(score, axis=1, keepdims=True)
        rows_kept[place] = jnp.broadcast_to(largest, (TILE, LANES))

    def weigh_tile(place, step):
        largest = jnp.concatenate([rows_kept[place]] * most_live, axis=1)
        weight = jnp.exp2((scores[place] - largest) * scale)
        weights[place] = weight.astype(jnp.bfloat16)
        denominators = jnp.sum(weight, axis=1, keepdims=True)
        rows_kept[place] = jnp.broadcast_to(1.0 / denominators, (TILE, LANES))

    def value_tile(place, step):
        values = [part(live, 2) for live in live_of(step)]
        total = jnp.dot(
            weights[place], jnp.concatenate(values, axis=0), preferred_element_type=jnp.float32
        )
        out_ref[step] = (total * rows_kept[place]).astype(out_ref.dtype)

    def some_tiles(first):
        for turn in range(together + 2 * APART):
            for behind, stage in enumerate((score_tile, weigh_tile, value_tile)):
                place = turn - behind * APART
                if 0 <= place < together:
                    stage(place, first + place)

    if tiles == together:
        some_tiles(0)
    else:

        def several(index, carry):
            some_tiles(index * together)
            return carry

        lax.fori_loop(0, tiles // together, several, 0)


def attend(gathered, factors, gains, lists, counts, base, tiles):
    device_count, _, tokens_here, head_width = gathered.shape
    most_live = lists.shape[1]
    tile_count = device_count * tokens_here // TILE
    blocks = -(-factors.shape[0] // LANES)
    factors = jnp.pad(factors, ((0, blocks * LANES - factors.shape[0]), (0, 0)))
    lists = lists.reshape(-1)
    counts = jnp.concatenate([counts, base.reshape(1)])
    together = max(size for size in range(1, max(1, 64 // most_live) + 1) if tiles % size == 0)
    anywhere = pl.BlockSpec(memory_space=pl.ANY)
    vmem = pl.BlockSpec(memory_space=pltpu.VMEM)
    return pl.pallas_call(
        functools.partial(attend_kernel, most_live),
        out_shape=jax.ShapeDtypeStruct((tiles, TILE, head_width), jnp.bfloat16),
        in_specs=[anywhere] * 2 + [vmem] * 3,
        out_specs=vmem,
        scratch_shapes=[
            pltpu.SMEM(lists.shape, jnp.int32),
            pltpu.SMEM(counts.shape, jnp.int32),
            pltpu.VMEM((blocks, LANES, LANES), jnp.float32),
            pltpu.VMEM((tile_count * TILE, head_width), jnp.bfloat16),
            pltpu.VMEM((tile_count * TILE, head_width), jnp.bfloat16),
            pltpu.VMEM((together, TILE, most_live * TILE), jnp.float32),
            pltpu.VMEM((together, TILE, most_live * TILE), jnp.bfloat16),
            pltpu.VMEM((together, TILE, LANES), jnp.float32),
            pltpu.SemaphoreType.DMA((2,)),
        ],
        compiler_params=pltpu.CompilerParams(vmem_limit_bytes=48 * 1024 * 1024),
        name="attend",
    )(lists, counts, factors, gains, gathered)


def squares_of(query, key):
    query, key = query.astype(jnp.float32), key.astype(jnp.float32)
    return jnp.stack([jnp.sum(query * query, axis=1), jnp.sum(key * key, axis=1)])


def swapped(held, reach, halves):
    count, width = lax.axis_size("seq"), lax.axis_size("tp")
    pairs = [(i * width + t, (i ^ reach) * width + t) for i in range(count) for t in halves]
    return lax.ppermute(held, ("seq", "tp"), pairs)


def doubled(held, reach, halves, across=None):
    other = swapped(held, across or reach, halves)
    upper = (lax.axis_index("seq") & reach) != 0
    first, second = jnp.where(upper, other, held), jnp.where(upper, held, other)
    return jnp.stack([first, second], axis=held.ndim - 2)


def local(query_proj, key_proj, value_proj, query_gain, key_gain, live_tiles, live_count):
    tokens_here = query_proj.shape[0]
    heads_here = live_tiles.shape[0]
    head_width = query_proj.shape[1] // heads_here
    full_width = query_proj.shape[1] * lax.axis_size("tp")
    device_count = lax.axis_size("seq")
    group_size = device_count // heads_here
    my_index = lax.axis_index("seq")
    my_head = my_index // group_size
    my_member = my_index % group_size

    outgoing = pack(query_proj, key_proj, value_proj, heads_here)
    halves = range(lax.axis_size("tp"))
    first_half = lax.axis_index("tp") == 0
    reaches = [1 << bit for bit in reversed(range((device_count - 1).bit_length()))]
    far, near = reaches[: len(reaches) // 2], reaches[len(reaches) // 2 :]
    spread = 1 << len(far)

    def gather_far(query, key):
        held = squares_of(query, key)
        for reach in far:
            held = doubled(held, reach, halves[:1], reach + sum(far[: far.index(reach)]))
        return held.reshape(spread, 2, tokens_here)

    def nothing(query, key):
        return jnp.zeros((spread, 2, tokens_here), jnp.float32)

    early = lax.cond(first_half, gather_far, nothing, query_proj, key_proj)
    outgoing, early = lax.optimization_barrier((outgoing, early))
    if group_size > 1:
        outgoing = jnp.repeat(outgoing, group_size, axis=0)
    gathered = lax.all_to_all(outgoing, "seq", split_axis=0, concat_axis=0, tiled=True)

    def rest_of_first(early, query, key):
        for reach in near:
            early = doubled(early, reach, halves[:1])
        return early.reshape(device_count, 2, tokens_here)

    def all_of_second(early, query, key):
        held = squares_of(query, key)
        for reach in near:
            held = doubled(held, reach, halves[1:])
        held = held.reshape(-1, 2, tokens_here)
        for reach in reversed(far):
            other = swapped(held, reach, halves[1:])
            upper = (my_index & reach) != 0
            held = jnp.concatenate(
                [jnp.where(upper, other, held), jnp.where(upper, held, other)], axis=0
            )
        return held

    held = lax.cond(first_half, rest_of_first, all_of_second, early, query_proj, key_proj)
    squares = held + lax.ppermute(held, "tp", [(0, 1), (1, 0)])
    factors = lax.rsqrt(squares / full_width + epsilon)
    tile_count = device_count * tokens_here // TILE
    factors = factors.transpose(1, 0, 2).reshape(2 * tile_count, TILE)
    gains = jnp.stack([query_gain, key_gain]).reshape(2, heads_here, head_width)
    gains = lax.dynamic_index_in_dim(gains, my_head, 1, keepdims=False)

    per_member = tile_count // group_size
    base = my_member * per_member
    lists = lax.dynamic_index_in_dim(live_tiles, my_head, 0, keepdims=False)
    counts = lax.dynamic_index_in_dim(live_count, my_head, 0, keepdims=False)
    lists = lax.dynamic_slice_in_dim(lists, base, per_member, 0)
    counts = lax.dynamic_slice_in_dim(counts, base, per_member, 0)
    results = attend(
        gathered, factors, gains, lists, counts, base.astype(jnp.int32), per_member
    )
    if group_size > 1:
        placed = jnp.zeros((tile_count, TILE, head_width), jnp.bfloat16)
        results = lax.dynamic_update_slice_in_dim(placed, results, base, 0)
    results = results.reshape(device_count, tokens_here, head_width)
    returned = lax.all_to_all(results, "seq", split_axis=0, concat_axis=0, tiled=True)
    if group_size > 1:
        returned = returned.reshape(heads_here, group_size, tokens_here, head_width)
        returned = returned.astype(jnp.float32).sum(axis=1).astype(jnp.bfloat16)
    returned = returned.reshape(heads_here, tokens_here // 8, 8, head_width)
    return returned.transpose(1, 2, 0, 3).reshape(tokens_here, heads_here * head_width)


def solution(mesh):
    placed = (
        P("seq", "tp"),
        P("seq", "tp"),
        P("seq", "tp"),
        P("tp"),
        P("tp"),
        P("tp", None, None),
        P("tp", None),
    )
    return jax.shard_map(
        local, mesh=mesh, in_specs=placed, out_specs=P("seq", "tp"), check_vma=False
    )
```
